32 devices in a mesh: expert: 16 (over z, y, core), tensor: 2 (over x).
Axes of the slice: x: 2, y: 2, z: 4, core: 2. Of those that a mesh axis runs over, the one named last changes fastest.
Arguments:
- tokens: bfloat16 [512, 7168], P(('expert', 'tensor')), may hold values from -6 to 6
- expert_ids: int32 [512, 8], P(('expert', 'tensor')), may hold values from 0 to 15, all different within a row; in each aligned block of 16 rows (0 to 15, 16 to 31, ...) at most 16 rows name the same one
- gate_values: float32 [512, 8], P(('expert', 'tensor')), may hold values from 0.05 to 0.6
- w_gate: bfloat16 [16, 7168, 1024], P('expert', None, 'tensor'), may hold values from -0.0625 to 0.0625
- w_up: bfloat16 [16, 7168, 1024], P('expert', None, 'tensor'), may hold values from -0.0625 to 0.0625
- w_down: bfloat16 [16, 1024, 7168], P('expert', 'tensor'), may hold values from -0.1875 to 0.1875
Outputs:
- mixed: bfloat16 [512, 7168], P(('expert', 'tensor'))
The draws below stay inside these ranges and needn't reach their ends.
Inputs may be any that keep to these rules, and one draw needn't show every extreme that they name: `expert_ids`: each row names 8 different experts; within each aligned block of 16 rows (the rows of one device) no expert is named by more than 16 rows.
All inputs are finite; a program needn't handle non-finite values.
Results may differ from the reference program's by a relative error of at most 0.012.
Values may be sent and summed in bfloat16 or wider, within the bound.
No kernel may reach another device: no remote copies, remote signals or barrier semaphores. Data moves between devices by JAX's collectives and lax.ppermute only.
A program may use at most 128 MiB of HBM per device.

```python
import math
import jax
import jax.numpy as jnp
import numpy as np
from jax import lax

D = 7168
FF = 1024
TOP = 8
TOK_DEV = 16
EXPERTS = 16
CAP = 16
TOKENS = 512
N_TENSOR = 2


def levels(rng, dims, cuts, smallest, largest):
    factor_of, own = 1.0, jax.random.fold_in(rng, 6)
    for axis_at, blocks in cuts:
        steps = jnp.exp(jax.random.uniform(jax.random.fold_in(own, axis_at), (blocks,), jnp.float32, smallest / len(cuts), largest / len(cuts)))
        factor_of = factor_of * jnp.repeat(steps, dims[axis_at] // blocks).reshape([-1 if axis == axis_at else 1 for axis in range(len(dims))])
    return factor_of


def shared_out(stream_key, own, number, rows, amount, top, limit, lean):
    sequence = jax.random.permutation(stream_key, amount)
    heavy_load, ordinary = shares(amount, rows * top, limit, lean, True), shares(amount, rows * top, limit, lean, False)
    places = jnp.arange(amount)

    def named(sizes, turn):
        used = int((sizes > 0).sum())
        fixed = max(1, used // 4)
        moved = fixed + (places - fixed + turn * (used - fixed)) % max(1, amount - fixed)
        return jnp.zeros((amount,), jnp.int32).at[sequence[jnp.where(places < fixed, places, moved)]].set(jnp.asarray(sizes, jnp.int32))

    sizes = jnp.where(number % 4 == 0, named(heavy_load, number // 4), named(ordinary, number - number // 4 - 1))
    mixed = jax.random.permutation(jax.random.fold_in(own, 3), amount)
    source_of, sink = mixed[0:amount // 2 * 2:2], mixed[1:amount // 2 * 2:2]
    slack = jnp.minimum(sizes[source_of] - 1, limit - sizes[sink]) // 2
    slack = jnp.where((source_of == sequence[0]) | (sink == sequence[0]) | (sizes[sink] == 0), 0, jnp.maximum(slack, 0))
    moved = jax.random.randint(jax.random.fold_in(own, 4), (amount // 2,), 0, 1 << 20) % (slack + 1)
    sizes = sizes.at[source_of].add(-moved).at[sink].add(moved)
    members = jnp.searchsorted(jnp.cumsum(sizes), jnp.arange(rows * top), side="right").astype(jnp.int32)
    listing = members.reshape(top, rows).T
    listing = listing[jax.random.permutation(jax.random.fold_in(own, 1), rows)]
    turn = jax.random.randint(jax.random.fold_in(own, 2), (rows, 1), 0, top)
    return jnp.take_along_axis(listing, (jnp.arange(top)[None, :] + turn) % top, axis=1)


def shares(count, total, most, lean, full):
    loads = [(1 << 20) // math.isqrt(rank ** lean) + 1 for rank in range(1, count + 1)]
    largest = most if full else min(most, max(-(-total // count), total * loads[0] // sum(loads)))
    least = 1 if total - largest >= count - 1 else 0
    counts, spare = [largest] + [least] * (count - 1), total - largest - least * (count - 1)
    while spare > 0:
        free = [i for i in range(1, count) if counts[i] < largest] or [i for i in range(1, count) if counts[i] < most]
        mass, budget = sum([loads[i] for i in free]), spare
        for i in free:
            more = min(most - counts[i], max(1, budget * loads[i] // mass), spare)
            counts[i] = counts[i] + more
            spare = spare - more
    return np.array(counts)


def gaussian(own_key, extent, deviation, most, cuts=(), kind=jnp.bfloat16):
    entries = jax.random.normal(own_key, extent, jnp.float32) * deviation
    if len(cuts) > 0:
        entries = levels(own_key, extent, cuts, -0.22, 0.18) * entries
    return jnp.clip(entries, min=-most, max=most).astype(kind)


def setup_inputs(seed: int = 0) -> dict:
    key_of = jax.random.split(jax.random.key(seed), 7)
    tokens = gaussian(key_of[0], (TOKENS, D), 1.0, 6.0, ((0, 32),))
    expert_ids_keys = jax.random.split(jax.random.fold_in(key_of[1], 1), TOKENS // TOK_DEV)
    expert_ids_turns = jax.random.permutation(jax.random.fold_in(key_of[1], 3), TOKENS // TOK_DEV)
    expert_ids = jax.vmap(lambda own, number: shared_out(jax.random.fold_in(key_of[1], 2), own, number, TOK_DEV, EXPERTS, TOP, CAP, 2))(expert_ids_keys, expert_ids_turns).reshape((TOKENS, TOP))
    gate_values = jnp.clip(0.05 + 0.55 * jax.random.uniform(key_of[2], (TOKENS, TOP), jnp.float32) ** levels(key_of[2], (TOKENS, TOP), ((0, 32),), -0.2, 0.2), 0.05, 0.6)
    w_gate = gaussian(key_of[3], (EXPERTS, D, FF), D ** -0.5, 0.0625, ((0, 16), (2, 2)))
    w_up = gaussian(key_of[4], (EXPERTS, D, FF), D ** -0.5, 0.0625, ((0, 16), (2, 2)))
    w_down = gaussian(key_of[5], (EXPERTS, FF, D), FF ** -0.5, 0.1875, ((0, 16), (1, 2)))
    return {"tokens": tokens, "expert_ids": expert_ids, "gate_values": gate_values, "w_gate": w_gate, "w_up": w_up, "w_down": w_down}


def reference(tokens, expert_ids, gate_values, w_gate, w_up, w_down):
    blocks = TOKENS // TOK_DEV
    pairs = expert_ids.reshape(blocks, TOK_DEV * TOP)
    onehot = (pairs[:, :, None] == jnp.arange(EXPERTS, dtype=jnp.int32)[None, None, :]).astype(jnp.int32)
    ranks = jnp.sum(jnp.cumsum(onehot, axis=1) * onehot, axis=2) - 1
    block_of = jnp.arange(blocks, dtype=jnp.int32)[:, None]
    flat_slot = pairs * (blocks * CAP) + block_of * CAP + ranks
    token_of = block_of * TOK_DEV + jnp.arange(TOK_DEV * TOP, dtype=jnp.int32)[None, :] // TOP
    table = jnp.zeros((EXPERTS * blocks * CAP,), jnp.int32).at[flat_slot.reshape(-1)].set(token_of.reshape(-1).astype(jnp.int32))
    weight_table = jnp.zeros((EXPERTS * blocks * CAP,), jnp.float32).at[flat_slot.reshape(-1)].set(gate_values.reshape(-1))
    width = FF // N_TENSOR

    def one_expert(total, inputs):
        index, weights, wg, wu, wd = inputs
        rows = tokens[index]
        gate = jnp.dot(rows, wg, preferred_element_type=jnp.float32)
        up = jnp.dot(rows, wu, preferred_element_type=jnp.float32)
        hidden = (jax.nn.silu(gate) * up).astype(jnp.bfloat16)
        summed = jnp.zeros((rows.shape[0], D), jnp.float32)
        for part in range(N_TENSOR):
            piece = jnp.dot(hidden[:, part * width:(part + 1) * width], wd[part * width:(part + 1) * width], preferred_element_type=jnp.float32)
            rounded = lax.optimization_barrier(piece.astype(jnp.bfloat16))
            summed = summed + rounded.astype(jnp.float32)
        out_rows = lax.optimization_barrier(summed.astype(jnp.bfloat16)).astype(jnp.float32)
        total = total.at[index].add(weights[:, None] * out_rows)
        return total, None

    start = jnp.zeros((TOKENS, D), jnp.float32)
    total, _ = lax.scan(one_expert, start, (table.reshape(EXPERTS, blocks * CAP), weight_table.reshape(EXPERTS, blocks * CAP), w_gate, w_up, w_down))
    return total.astype(jnp.bfloat16)
```

```python
import jax
import jax.numpy as jnp
from jax import lax
from jax.sharding import PartitionSpec as P

AXES = ("expert", "tensor")


def slot_places(expert_ids, experts, capacity):
    count = expert_ids.shape[0] * expert_ids.shape[1]
    flat = expert_ids.reshape(count)
    onehot = (flat[:, None] == jnp.arange(experts, dtype=jnp.int32)[None, :]).astype(jnp.int32)
    ranks = jnp.sum(jnp.cumsum(onehot, axis=0) * onehot, axis=1) - 1
    return flat * capacity + ranks


def dispatch_rows(tokens, places, experts, capacity, top):
    count = tokens.shape[0]
    table = (places[:, None] == jnp.arange(experts * capacity, dtype=jnp.int32)[None, :]).astype(
        jnp.bfloat16
    )
    table = jnp.sum(table.reshape(count, top, experts * capacity), axis=1)
    rows = jnp.einsum("ns,nd->sd", table, tokens, preferred_element_type=jnp.float32)
    return rows.astype(jnp.bfloat16).reshape(experts, capacity, tokens.shape[1])


def swiglu(rows, wg, wu):
    gate = jnp.dot(rows, wg, preferred_element_type=jnp.float32)
    up = jnp.dot(rows, wu, preferred_element_type=jnp.float32)
    return (jax.nn.silu(gate) * up).astype(jnp.bfloat16)


def slotted(tokens, expert_ids, gate_values, w_gate, w_up, w_down, capacity):
    experts = lax.axis_size("expert")
    count, top = expert_ids.shape
    width = tokens.shape[1]
    places = slot_places(expert_ids, experts, capacity)
    sending = dispatch_rows(tokens, places, experts, capacity, top)
    arrived = lax.all_to_all(sending, "expert", split_axis=0, concat_axis=0, tiled=True)
    rows = arrived.reshape(experts * capacity, width)
    hidden = swiglu(lax.all_gather(rows, "tensor", axis=0, tiled=True), w_gate[0], w_up[0])
    summed = lax.psum_scatter(
        jnp.dot(hidden, w_down[0], preferred_element_type=jnp.float32).astype(jnp.bfloat16),
        "tensor",
        scatter_dimension=0,
        tiled=True,
    )
    out_rows = summed.reshape(experts, capacity, width)
    returned = lax.all_to_all(out_rows, "expert", split_axis=0, concat_axis=0, tiled=True)
    picked = returned.reshape(experts * capacity, width)[places].reshape(count, top, width)
    mixed = jnp.sum(gate_values[:, :, None] * picked.astype(jnp.float32), axis=1)
    return mixed.astype(jnp.bfloat16)


def expert_weights(expert_ids, gate_values, experts):
    named = expert_ids[:, :, None] == jnp.arange(experts, dtype=jnp.int32)[None, None, :]
    return jnp.sum(jnp.where(named, gate_values[:, :, None], 0.0), axis=1)


def dense(tokens, expert_ids, gate_values, w_gate, w_up, w_down):
    experts = lax.axis_size("expert")
    weights = expert_weights(expert_ids, gate_values, experts)
    rows = lax.all_gather(tokens, AXES, axis=0, tiled=True)
    weights = lax.all_gather(weights, AXES, axis=0, tiled=True)
    mine = lax.dynamic_slice_in_dim(weights, lax.axis_index("expert"), 1, axis=1)
    hidden = swiglu(rows, w_gate[0], w_up[0])
    partial = mine * jnp.dot(hidden, w_down[0], preferred_element_type=jnp.float32)
    return lax.psum_scatter(partial.astype(jnp.bfloat16), AXES, scatter_dimension=0, tiled=True)


def local(tokens, expert_ids, gate_values, w_gate, w_up, w_down):
    experts = lax.axis_size("expert")
    count, top = expert_ids.shape
    capacity = min(count, max(2, 2 * count * top // experts))
    if capacity < count:
        return slotted(tokens, expert_ids, gate_values, w_gate, w_up, w_down, capacity)
    return dense(tokens, expert_ids, gate_values, w_gate, w_up, w_down)


def solution(mesh):
    return jax.shard_map(
        local,
        mesh=mesh,
        in_specs=(
            P(("expert", "tensor"), None),
            P(("expert", "tensor"), None),
            P(("expert", "tensor"), None),
            P("expert", None, "tensor"),
            P("expert", None, "tensor"),
            P("expert", "tensor", None),
        ),
        out_specs=P(("expert", "tensor"), None),
        check_vma=False,
    )
```

```python
import jax
import jax.numpy as jnp
from jax import lax
from jax.sharding import PartitionSpec as P

AXES = ("expert", "tensor")
CHUNKS = 2


def slot_places(expert_ids, experts, capacity):
    count = expert_ids.shape[0] * expert_ids.shape[1]
    flat = expert_ids.reshape(count)
    onehot = (flat[:, None] == jnp.arange(experts, dtype=jnp.int32)[None, :]).astype(jnp.int32)
    ranks = jnp.sum(jnp.cumsum(onehot, axis=0) * onehot, axis=1) - 1
    return flat * capacity + ranks


def dispatch_rows(tokens, places, experts, capacity, top):
    count = tokens.shape[0]
    table = (places[:, None] == jnp.arange(experts * capacity, dtype=jnp.int32)[None, :]).astype(
        jnp.bfloat16
    )
    table = jnp.sum(table.reshape(count, top, experts * capacity), axis=1)
    rows = jnp.einsum("ns,nd->sd", table, tokens, preferred_element_type=jnp.float32)
    return rows.astype(jnp.bfloat16).reshape(experts, capacity, tokens.shape[1])


def swiglu(rows, wg, wu):
    gate = jnp.dot(rows, wg, preferred_element_type=jnp.float32)
    up = jnp.dot(rows, wu, preferred_element_type=jnp.float32)
    return (jax.nn.silu(gate) * up).astype(jnp.bfloat16)


def slotted(tokens, expert_ids, gate_values, w_gate, w_up, w_down, capacity):
    experts = lax.axis_size("expert")
    count, top = expert_ids.shape
    width = tokens.shape[1]
    places = slot_places(expert_ids, experts, capacity)
    sending = dispatch_rows(tokens, places, experts, capacity, top)
    arrived = lax.all_to_all(sending, "expert", split_axis=0, concat_axis=0, tiled=True)
    rows = arrived.reshape(experts * capacity, width)
    hidden = swiglu(lax.all_gather(rows, "tensor", axis=0, tiled=True), w_gate[0], w_up[0])
    summed = lax.psum_scatter(
        jnp.dot(hidden, w_down[0], preferred_element_type=jnp.float32).astype(jnp.bfloat16),
        "tensor",
        scatter_dimension=0,
        tiled=True,
    )
    out_rows = summed.reshape(experts, capacity, width)
    returned = lax.all_to_all(out_rows, "expert", split_axis=0, concat_axis=0, tiled=True)
    picked = returned.reshape(experts * capacity, width)[places].reshape(count, top, width)
    mixed = jnp.sum(gate_values[:, :, None] * picked.astype(jnp.float32), axis=1)
    return mixed.astype(jnp.bfloat16)


def expert_weights(expert_ids, gate_values, experts):
    named = expert_ids[:, :, None] == jnp.arange(experts, dtype=jnp.int32)[None, None, :]
    return jnp.sum(jnp.where(named, gate_values[:, :, None], 0.0), axis=1)


def swap(pairs):
    experts, parts = lax.axis_size("expert"), lax.axis_size("tensor")
    perm = []
    for e in range(experts):
        for t in range(parts):
            to = pairs(e, t)
            perm.append((e * parts + t, to[0] * parts + to[1]))
    return perm


def step_core():
    return swap(lambda e, t: (e ^ 1, t))


def step_first():
    return swap(lambda e, t: (e ^ 2, t) if e % 2 else (e, t ^ 1))


def step_second():
    return swap(lambda e, t: (e, t ^ 1) if e % 2 else (e ^ 2, t))


def step_line(back):
    experts = lax.axis_size("expert")
    return swap(lambda e, t: ((e - 4 * back) % experts, t))


def gather_rows(block):
    lines = lax.axis_size("expert") // 4
    rows = [block] + [lax.ppermute(block, AXES, step_line(k)) for k in range(1, lines)]
    rows = jnp.concatenate(rows, axis=0)
    for step in (step_second, step_first, step_core):
        rows = jnp.concatenate([rows, lax.ppermute(rows, AXES, step())], axis=0)
    return rows


def half_sum(partial, step):
    half = partial.shape[0] // 2
    arrived = lax.ppermute(partial[half:], AXES, step())
    return (partial[:half].astype(jnp.float32) + arrived.astype(jnp.float32)).astype(jnp.bfloat16)


def scatter_rows(partial):
    lines = lax.axis_size("expert") // 4
    for step in (step_core, step_first, step_second):
        partial = half_sum(partial, step)
    count = partial.shape[0] // lines
    total = partial[:count].astype(jnp.float32)
    for k in range(1, lines):
        block = partial[k * count : (k + 1) * count]
        total = total + lax.ppermute(block, AXES, step_line(-k)).astype(jnp.float32)
    return total.astype(jnp.bfloat16)


def cuts(width, pieces):
    tiles = width // 128
    edges = [128 * (tiles * i // pieces) for i in range(pieces)] + [width]
    return list(zip(edges[:-1], edges[1:]))


def dense(tokens, expert_ids, gate_values, w_gate, w_up, w_down):
    experts = lax.axis_size("expert")
    count, width = tokens.shape
    weights = expert_weights(expert_ids, gate_values, experts)
    high = lax.reduce_precision(weights, 8, 7)
    packed = jnp.concatenate([high, weights - high], axis=1).astype(jnp.bfloat16)
    packed = jnp.pad(packed, ((0, 0), (0, -2 * experts % 128)))
    chunks = cuts(width, CHUNKS)
    gate = up = 0.0
    for i, (lo, hi) in enumerate(chunks):
        block = tokens[:, lo:hi]
        if i == 0:
            block = jnp.concatenate([block, packed], axis=1)
        rows = gather_rows(block)
        if i == 0:
            spread = rows[:, hi - lo :]
            rows = rows[:, : hi - lo]
        gate = gate + jnp.dot(rows, w_gate[0, lo:hi], preferred_element_type=jnp.float32)
        up = up + jnp.dot(rows, w_up[0, lo:hi], preferred_element_type=jnp.float32)
    hidden = (jax.nn.silu(gate) * up).astype(jnp.bfloat16)
    me = lax.axis_index("expert")
    column = jnp.arange(spread.shape[1], dtype=jnp.int32)
    named = (column == me) | (column == me + experts)
    mine = jnp.sum(jnp.where(named[None, :], spread.astype(jnp.float32), 0.0), axis=1, keepdims=True)
    outs = []
    for lo, hi in chunks:
        partial = mine * jnp.dot(hidden, w_down[0, :, lo:hi], preferred_element_type=jnp.float32)
        outs.append(scatter_rows(partial.astype(jnp.bfloat16)))
    return jnp.concatenate(outs, axis=1)


def local(tokens, expert_ids, gate_values, w_gate, w_up, w_down):
    experts = lax.axis_size("expert")
    count, top = expert_ids.shape
    capacity = min(count, max(2, 2 * count * top // experts))
    if capacity < count or experts % 4 or lax.axis_size("tensor") != 2:
        return slotted(tokens, expert_ids, gate_values, w_gate, w_up, w_down, capacity)
    return dense(tokens, expert_ids, gate_values, w_gate, w_up, w_down)


def solution(mesh):
    return jax.shard_map(
        local,
        mesh=mesh,
        in_specs=(
            P(("expert", "tensor"), None),
            P(("expert", "tensor"), None),
            P(("expert", "tensor"), None),
            P("expert", None, "tensor"),
            P("expert", None, "tensor"),
            P("expert", "tensor", None),
        ),
        out_specs=P(("expert", "tensor"), None),
        check_vma=False,
    )
```

```python
import jax
import jax.numpy as jnp
from jax import lax
from jax.sharding import PartitionSpec as P

AXES = ("expert", "tensor")


def slot_places(expert_ids, experts, capacity):
    count = expert_ids.shape[0] * expert_ids.shape[1]
    flat = expert_ids.reshape(count)
    onehot = (flat[:, None] == jnp.arange(experts, dtype=jnp.int32)[None, :]).astype(jnp.int32)
    ranks = jnp.sum(jnp.cumsum(onehot, axis=0) * onehot, axis=1) - 1
    return flat * capacity + ranks


def dispatch_rows(tokens, places, experts, capacity, top):
    count = tokens.shape[0]
    table = (places[:, None] == jnp.arange(experts * capacity, dtype=jnp.int32)[None, :]).astype(
        jnp.bfloat16
    )
    table = jnp.sum(table.reshape(count, top, experts * capacity), axis=1)
    rows = jnp.einsum("ns,nd->sd", table, tokens, preferred_element_type=jnp.float32)
    return rows.astype(jnp.bfloat16).reshape(experts, capacity, tokens.shape[1])


def swiglu(rows, wg, wu):
    gate = jnp.dot(rows, wg, preferred_element_type=jnp.float32)
    up = jnp.dot(rows, wu, preferred_element_type=jnp.float32)
    return (jax.nn.silu(gate) * up).astype(jnp.bfloat16)


def slotted(tokens, expert_ids, gate_values, w_gate, w_up, w_down, capacity):
    experts = lax.axis_size("expert")
    count, top = expert_ids.shape
    width = tokens.shape[1]
    places = slot_places(expert_ids, experts, capacity)
    sending = dispatch_rows(tokens, places, experts, capacity, top)
    arrived = lax.all_to_all(sending, "expert", split_axis=0, concat_axis=0, tiled=True)
    rows = arrived.reshape(experts * capacity, width)
    hidden = swiglu(lax.all_gather(rows, "tensor", axis=0, tiled=True), w_gate[0], w_up[0])
    summed = lax.psum_scatter(
        jnp.dot(hidden, w_down[0], preferred_element_type=jnp.float32).astype(jnp.bfloat16),
        "tensor",
        scatter_dimension=0,
        tiled=True,
    )
    out_rows = summed.reshape(experts, capacity, width)
    returned = lax.all_to_all(out_rows, "expert", split_axis=0, concat_axis=0, tiled=True)
    picked = returned.reshape(experts * capacity, width)[places].reshape(count, top, width)
    mixed = jnp.sum(gate_values[:, :, None] * picked.astype(jnp.float32), axis=1)
    return mixed.astype(jnp.bfloat16)


def expert_weights(expert_ids, gate_values, experts):
    named = expert_ids[:, :, None] == jnp.arange(experts, dtype=jnp.int32)[None, None, :]
    return jnp.sum(jnp.where(named, gate_values[:, :, None], 0.0), axis=1)


def partner(step, e, t):
    if step == "core":
        return e ^ 1, t
    if step == "far":
        return e ^ 8, t
    if step == "near":
        return e ^ 4, t
    return (e, t ^ 1) if (e & 1) == (step == "late") else (e ^ 2, t)


def exchange(block, step):
    parts = lax.axis_size("tensor")
    perm = []
    for e in range(lax.axis_size("expert")):
        for t in range(parts):
            other = partner(step, e, t)
            perm.append((e * parts + t, other[0] * parts + other[1]))
    return lax.ppermute(block, AXES, perm)


STEPS = ("far", "near", "late", "early")
PLAN = (
    (20, ("near", "far", "early", "late")),
    (20, ("far", "early", "late", "near")),
    (16, ("far", "early", "near", "late")),
)


def chunks_of(width):
    tiles, total = width // 128, sum(share for share, _ in PLAN)
    edges, at = [0], 0
    for share, _ in PLAN:
        at += share
        edges.append(128 * (tiles * at // total))
    return [(lo, hi, order) for lo, hi, (_, order) in zip(edges[:-1], edges[1:], PLAN)]


def gather_rows(block, order):
    count, width = block.shape
    rows = block.reshape(1, 1, 1, 1, count, width)
    for step in order:
        rows = jnp.concatenate([rows, exchange(rows, step)], axis=STEPS.index(step))
    rows = rows.reshape(-1, width)
    return rows, exchange(rows, "core")


def scatter_rows(kept, sent, order):
    count, width = kept.shape
    total = kept + exchange(sent.astype(jnp.bfloat16), "core").astype(jnp.float32)
    total = total.reshape(2, 2, 2, 2, count // 16, width)
    for step in reversed(order):
        axis = STEPS.index(step)
        total = total.astype(jnp.bfloat16)
        mine, other = lax.slice_in_dim(total, 0, 1, axis=axis), lax.slice_in_dim(total, 1, 2, axis=axis)
        total = mine.astype(jnp.float32) + exchange(other, step).astype(jnp.float32)
    return total.astype(jnp.bfloat16).reshape(count // 16, width)


def dense(tokens, expert_ids, gate_values, w_gate, w_up, w_down):
    experts = lax.axis_size("expert")
    count, width = tokens.shape
    weights = expert_weights(expert_ids, gate_values, experts)
    high = lax.reduce_precision(weights, 8, 7)
    packed = jnp.concatenate([high, weights - high], axis=1).astype(jnp.bfloat16)
    packed = jnp.pad(packed, ((0, 0), (0, -2 * experts % 128)))
    chunks = chunks_of(width)
    gates, ups = [0.0, 0.0], [0.0, 0.0]
    for i, (lo, hi, order) in enumerate(chunks):
        block = tokens[:, lo:hi]
        last = i == len(chunks) - 1
        if last:
            block = jnp.concatenate([block, packed], axis=1)
        halves = gather_rows(block, order)
        if last:
            spread = [rows[:, hi - lo :] for rows in halves]
            halves = [rows[:, : hi - lo] for rows in halves]
        for j, rows in enumerate(halves):
            gates[j] = gates[j] + jnp.dot(rows, w_gate[0, lo:hi], preferred_element_type=jnp.float32)
            ups[j] = ups[j] + jnp.dot(rows, w_up[0, lo:hi], preferred_element_type=jnp.float32)
    hidden = [(jax.nn.silu(gate) * up).astype(jnp.bfloat16) for gate, up in zip(gates, ups)]
    me = lax.axis_index("expert")
    column = jnp.arange(spread[0].shape[1], dtype=jnp.int32)
    named = (column == me) | (column == me + experts)
    scale = [
        jnp.sum(jnp.where(named[None, :], rows.astype(jnp.float32), 0.0), axis=1, keepdims=True)
        for rows in spread
    ]
    outs = []
    for lo, hi, order in chunks:
        sent, kept = [
            scale[j] * jnp.dot(hidden[j], w_down[0, :, lo:hi], preferred_element_type=jnp.float32)
            for j in (1, 0)
        ]
        outs.append(scatter_rows(kept, sent, order))
    return jnp.concatenate(outs, axis=1)


def local(tokens, expert_ids, gate_values, w_gate, w_up, w_down):
    experts = lax.axis_size("expert")
    count, top = expert_ids.shape
    capacity = min(count, max(2, 2 * count * top // experts))
    if capacity < count or experts != 16 or lax.axis_size("tensor") != 2:
        return slotted(tokens, expert_ids, gate_values, w_gate, w_up, w_down, capacity)
    return dense(tokens, expert_ids, gate_values, w_gate, w_up, w_down)


def solution(mesh):
    return jax.shard_map(
        local,
        mesh=mesh,
        in_specs=(
            P(("expert", "tensor"), None),
            P(("expert", "tensor"), None),
            P(("expert", "tensor"), None),
            P("expert", None, "tensor"),
            P("expert", None, "tensor"),
            P("expert", "tensor", None),
        ),
        out_specs=P(("expert", "tensor"), None),
        check_vma=False,
    )
```

```python
import jax
import jax.numpy as jnp
from jax import lax
from jax.sharding import PartitionSpec as P

AXES = ("expert", "tensor")


def slot_places(expert_ids, experts, capacity):
    count = expert_ids.shape[0] * expert_ids.shape[1]
    flat = expert_ids.reshape(count)
    onehot = (flat[:, None] == jnp.arange(experts, dtype=jnp.int32)[None, :]).astype(jnp.int32)
    ranks = jnp.sum(jnp.cumsum(onehot, axis=0) * onehot, axis=1) - 1
    return flat * capacity + ranks


def dispatch_rows(tokens, places, experts, capacity, top):
    count = tokens.shape[0]
    table = (places[:, None] == jnp.arange(experts * capacity, dtype=jnp.int32)[None, :]).astype(
        jnp.bfloat16
    )
    table = jnp.sum(table.reshape(count, top, experts * capacity), axis=1)
    rows = jnp.einsum("ns,nd->sd", table, tokens, preferred_element_type=jnp.float32)
    return rows.astype(jnp.bfloat16).reshape(experts, capacity, tokens.shape[1])


def swiglu(rows, wg, wu):
    gate = jnp.dot(rows, wg, preferred_element_type=jnp.float32)
    up = jnp.dot(rows, wu, preferred_element_type=jnp.float32)
    return (jax.nn.silu(gate) * up).astype(jnp.bfloat16)


def slotted(tokens, expert_ids, gate_values, w_gate, w_up, w_down, capacity):
    experts = lax.axis_size("expert")
    count, top = expert_ids.shape
    width = tokens.shape[1]
    places = slot_places(expert_ids, experts, capacity)
    sending = dispatch_rows(tokens, places, experts, capacity, top)
    arrived = lax.all_to_all(sending, "expert", split_axis=0, concat_axis=0, tiled=True)
    rows = arrived.reshape(experts * capacity, width)
    hidden = swiglu(lax.all_gather(rows, "tensor", axis=0, tiled=True), w_gate[0], w_up[0])
    summed = lax.psum_scatter(
        jnp.dot(hidden, w_down[0], preferred_element_type=jnp.float32).astype(jnp.bfloat16),
        "tensor",
        scatter_dimension=0,
        tiled=True,
    )
    out_rows = summed.reshape(experts, capacity, width)
    returned = lax.all_to_all(out_rows, "expert", split_axis=0, concat_axis=0, tiled=True)
    picked = returned.reshape(experts * capacity, width)[places].reshape(count, top, width)
    mixed = jnp.sum(gate_values[:, :, None] * picked.astype(jnp.float32), axis=1)
    return mixed.astype(jnp.bfloat16)


def expert_weights(expert_ids, gate_values, experts):
    named = expert_ids[:, :, None] == jnp.arange(experts, dtype=jnp.int32)[None, None, :]
    return jnp.sum(jnp.where(named, gate_values[:, :, None], 0.0), axis=1)


def partner(step, e, t):
    if step == "core":
        return e ^ 1, t
    if step == "far":
        return e ^ 8, t
    if step == "near":
        return e ^ 4, t
    return (e, t ^ 1) if (e & 1) == (step == "late") else (e ^ 2, t)


def exchange(block, step):
    parts = lax.axis_size("tensor")
    perm = []
    for e in range(lax.axis_size("expert")):
        for t in range(parts):
            other = partner(step, e, t)
            perm.append((e * parts + t, other[0] * parts + other[1]))
    return lax.ppermute(block, AXES, perm)


STEPS = ("far", "near", "late", "early")
GATHER = (
    (20, ("near", "far", "early", "late")),
    (20, ("far", "early", "late", "near")),
    (16, ("far", "early", "near", "late")),
)
SCATTER = (
    (16, ("late", "far", "early", "near")),
    (20, ("near", "late", "early", "far")),
    (20, ("late", "early", "far", "near")),
)
TURNS = (0, 1, 2, 0, 2, 1, 2, 0, 1, 0, 1, 2, 0, 1, 2)


def chunks_of(width, plan):
    tiles, total = width // 128, sum(share for share, _ in plan)
    edges, at = [0], 0
    for share, _ in plan:
        at += share
        edges.append(128 * (tiles * at // total))
    return [(lo, hi, order) for lo, hi, (_, order) in zip(edges[:-1], edges[1:], plan)]


def gather_rows(block, order):
    count, width = block.shape
    rows = block.reshape(1, 1, 1, 1, count, width)
    for step in order:
        rows = jnp.concatenate([rows, exchange(rows, step)], axis=STEPS.index(step))
    rows = rows.reshape(-1, width)
    return rows, exchange(rows, "core")


def scatter_rows(hidden, scale, w_down, chunks):
    def product(j, chunk):
        lo, hi, _ = chunk
        return scale[j] * jnp.dot(hidden[j], w_down[:, lo:hi], preferred_element_type=jnp.float32)

    state = [[exchange(product(1, chunk).astype(jnp.bfloat16), "core"), None, 0] for chunk in chunks]
    before = hidden[0]
    count = hidden[0].shape[0] // 16
    outs = [None] * len(chunks)
    for k in TURNS:
        arrived, mine, done = state[k]
        lo, hi, order = chunks[k]
        arrived, before = lax.optimization_barrier((arrived, before))
        if done == 0:
            total = product(0, chunks[k]) + arrived.astype(jnp.float32)
            total = total.reshape(2, 2, 2, 2, count, hi - lo).astype(jnp.bfloat16)
        else:
            total = (mine.astype(jnp.float32) + arrived.astype(jnp.float32)).astype(jnp.bfloat16)
        before = total
        if done == len(order):
            outs[k] = total.reshape(count, hi - lo)
            continue
        axis = STEPS.index(order[done])
        mine, other = lax.slice_in_dim(total, 0, 1, axis=axis), lax.slice_in_dim(total, 1, 2, axis=axis)
        state[k] = [exchange(other, order[done]), mine, done + 1]
    return jnp.concatenate(outs, axis=1)


def dense(tokens, expert_ids, gate_values, w_gate, w_up, w_down):
    experts = lax.axis_size("expert")
    count, width = tokens.shape
    weights = expert_weights(expert_ids, gate_values, experts)
    high = lax.reduce_precision(weights, 8, 7)
    packed = jnp.concatenate([high, weights - high], axis=1).astype(jnp.bfloat16)
    packed = jnp.pad(packed, ((0, 0), (0, -2 * experts % 128)))
    chunks = chunks_of(width, GATHER)
    gates, ups = [0.0, 0.0], [0.0, 0.0]
    for i, (lo, hi, order) in enumerate(chunks):
        block = tokens[:, lo:hi]
        last = i == len(chunks) - 1
        if last:
            block = jnp.concatenate([block, packed], axis=1)
        halves = gather_rows(block, order)
        if last:
            spread = [rows[:, hi - lo :] for rows in halves]
            halves = [rows[:, : hi - lo] for rows in halves]
        for j, rows in enumerate(halves):
            gates[j] = gates[j] + jnp.dot(rows, w_gate[0, lo:hi], preferred_element_type=jnp.float32)
            ups[j] = ups[j] + jnp.dot(rows, w_up[0, lo:hi], preferred_element_type=jnp.float32)
    hidden = [(jax.nn.silu(gate) * up).astype(jnp.bfloat16) for gate, up in zip(gates, ups)]
    me = lax.axis_index("expert")
    column = jnp.arange(spread[0].shape[1], dtype=jnp.int32)
    named = (column == me) | (column == me + experts)
    scale = [
        jnp.sum(jnp.where(named[None, :], rows.astype(jnp.float32), 0.0), axis=1, keepdims=True)
        for rows in spread
    ]
    return scatter_rows(hidden, scale, w_down[0], chunks_of(width, SCATTER))


def local(tokens, expert_ids, gate_values, w_gate, w_up, w_down):
    experts = lax.axis_size("expert")
    count, top = expert_ids.shape
    capacity = min(count, max(2, 2 * count * top // experts))
    if capacity < count or experts != 16 or lax.axis_size("tensor") != 2:
        return slotted(tokens, expert_ids, gate_values, w_gate, w_up, w_down, capacity)
    return dense(tokens, expert_ids, gate_values, w_gate, w_up, w_down)


def solution(mesh):
    return jax.shard_map(
        local,
        mesh=mesh,
        in_specs=(
            P(("expert", "tensor"), None),
            P(("expert", "tensor"), None),
            P(("expert", "tensor"), None),
            P("expert", None, "tensor"),
            P("expert", None, "tensor"),
            P("expert", "tensor", None),
        ),
        out_specs=P(("expert", "tensor"), None),
        check_vma=False,
    )
```

```python
import jax
import jax.numpy as jnp
from jax import lax
from jax.sharding import PartitionSpec as P

AXES = ("expert", "tensor")


def slot_places(expert_ids, experts, capacity):
    count = expert_ids.shape[0] * expert_ids.shape[1]
    flat = expert_ids.reshape(count)
    onehot = (flat[:, None] == jnp.arange(experts, dtype=jnp.int32)[None, :]).astype(jnp.int32)
    ranks = jnp.sum(jnp.cumsum(onehot, axis=0) * onehot, axis=1) - 1
    return flat * capacity + ranks


def dispatch_rows(tokens, places, experts, capacity, top):
    count = tokens.shape[0]
    table = (places[:, None] == jnp.arange(experts * capacity, dtype=jnp.int32)[None, :]).astype(
        jnp.bfloat16
    )
    table = jnp.sum(table.reshape(count, top, experts * capacity), axis=1)
    rows = jnp.einsum("ns,nd->sd", table, tokens, preferred_element_type=jnp.float32)
    return rows.astype(jnp.bfloat16).reshape(experts, capacity, tokens.shape[1])


def swiglu(rows, wg, wu):
    gate = jnp.dot(rows, wg, preferred_element_type=jnp.float32)
    up = jnp.dot(rows, wu, preferred_element_type=jnp.float32)
    return (jax.nn.silu(gate) * up).astype(jnp.bfloat16)


def slotted(tokens, expert_ids, gate_values, w_gate, w_up, w_down, capacity):
    experts = lax.axis_size("expert")
    count, top = expert_ids.shape
    width = tokens.shape[1]
    places = slot_places(expert_ids, experts, capacity)
    sending = dispatch_rows(tokens, places, experts, capacity, top)
    arrived = lax.all_to_all(sending, "expert", split_axis=0, concat_axis=0, tiled=True)
    rows = arrived.reshape(experts * capacity, width)
    hidden = swiglu(lax.all_gather(rows, "tensor", axis=0, tiled=True), w_gate[0], w_up[0])
    summed = lax.psum_scatter(
        jnp.dot(hidden, w_down[0], preferred_element_type=jnp.float32).astype(jnp.bfloat16),
        "tensor",
        scatter_dimension=0,
        tiled=True,
    )
    out_rows = summed.reshape(experts, capacity, width)
    returned = lax.all_to_all(out_rows, "expert", split_axis=0, concat_axis=0, tiled=True)
    picked = returned.reshape(experts * capacity, width)[places].reshape(count, top, width)
    mixed = jnp.sum(gate_values[:, :, None] * picked.astype(jnp.float32), axis=1)
    return mixed.astype(jnp.bfloat16)


def expert_weights(expert_ids, gate_values, experts):
    named = expert_ids[:, :, None] == jnp.arange(experts, dtype=jnp.int32)[None, None, :]
    return jnp.sum(jnp.where(named, gate_values[:, :, None], 0.0), axis=1)


def partner(step, e, t):
    if step == "core":
        return e ^ 1, t
    if step in ("far", "near"):
        return (e ^ 4, t) if (e & 1) == (step == "far") else (e ^ 8, t)
    return (e, t ^ 1) if (e & 1) == (step == "late") else (e ^ 2, t)


def exchange(block, step):
    parts = lax.axis_size("tensor")
    perm = []
    for e in range(lax.axis_size("expert")):
        for t in range(parts):
            other = partner(step, e, t)
            perm.append((e * parts + t, other[0] * parts + other[1]))
    return lax.ppermute(block, AXES, perm)


STEPS = ("far", "near", "late", "early")
GATHER = (
    (18, ("near", "far", "early", "late")),
    (20, ("early", "near", "far", "late")),
    (18, ("near", "early", "late", "far")),
)
SCATTER = (
    (20, ("late", "early", "near", "far")),
    (20, ("near", "late", "early", "far")),
    (16, ("late", "early", "far", "near")),
)
GATHER_TURNS = (10, 11, 12, 10, 11, 12, 12, 10, 11, 12, 10, 11, 10, 10, 10, 11, 11, 12, 12, 11, 12)
SCATTER_TURNS = (0, 1, 2, 0, 2, 1, 0, 2, 1, 0, 2, 1, 0, 2, 1)
PACKED = 2


def chunks_of(width, plan):
    tiles, total = width // 128, sum(share for share, _ in plan)
    edges, at = [0], 0
    for share, _ in plan:
        at += share
        edges.append(128 * (tiles * at // total))
    return [(lo, hi, order) for lo, hi, (_, order) in zip(edges[:-1], edges[1:], plan)]


def gather_rows(tokens, packed, w_gate, w_up, chunks):
    count, width = tokens.shape
    blocks = [tokens[:, lo:hi] for lo, hi, _ in chunks]
    blocks[PACKED] = jnp.concatenate([blocks[PACKED], packed], axis=1)
    state = [[block.reshape(1, 1, 1, 1, count, -1), None, 0] for block in blocks]
    before = tokens
    gates, ups, spread = [0.0, 0.0], [0.0, 0.0], [None, None]

    def products(k, j, rows):
        lo, hi, _ = chunks[k]
        if k == PACKED:
            spread[j], rows = rows[:, hi - lo :], rows[:, : hi - lo]
        gates[j] = gates[j] + jnp.dot(rows, w_gate[lo:hi], preferred_element_type=jnp.float32)
        ups[j] = ups[j] + jnp.dot(rows, w_up[lo:hi], preferred_element_type=jnp.float32)
        return ups[j]

    for k in GATHER_TURNS:
        free, k = k >= 10, k % 10
        rows, arrived, done = state[k]
        order = chunks[k][2]
        if free:
            pass
        elif done > 0 and done != len(order) + 1:
            arrived, before = lax.optimization_barrier((arrived, before))
        elif done > 0:
            rows, before = lax.optimization_barrier((rows, before))
        if 0 < done <= len(order):
            rows = jnp.concatenate([rows, arrived], axis=STEPS.index(order[done - 1]))
            before = rows
        if done < len(order):
            arrived = exchange(rows, order[done])
        elif done == len(order):
            rows = rows.reshape(16 * count, -1)
            arrived = exchange(rows, "core")
        elif done == len(order) + 1:
            before = products(k, 0, rows)
        else:
            before = products(k, 1, arrived)
        state[k] = [rows, arrived, done + 1]
    return gates, ups, spread


def scatter_rows(hidden, scale, w_down, chunks):
    def product(j, chunk):
        lo, hi, _ = chunk
        return scale[j] * jnp.dot(hidden[j], w_down[:, lo:hi], preferred_element_type=jnp.float32)

    state = [[exchange(product(1, chunk).astype(jnp.bfloat16), "core"), None, 0] for chunk in chunks]
    before = hidden[0]
    count = hidden[0].shape[0] // 16
    outs = [None] * len(chunks)
    for k in SCATTER_TURNS:
        free, k = k >= 10, k % 10
        arrived, mine, done = state[k]
        lo, hi, order = chunks[k]
        if not free:
            arrived, before = lax.optimization_barrier((arrived, before))
        if done == 0:
            total = product(0, chunks[k]) + arrived.astype(jnp.float32)
            total = total.reshape(2, 2, 2, 2, count, hi - lo).astype(jnp.bfloat16)
        else:
            total = (mine.astype(jnp.float32) + arrived.astype(jnp.float32)).astype(jnp.bfloat16)
        before = total
        if done == len(order):
            outs[k] = total.reshape(count, hi - lo)
            continue
        axis = STEPS.index(order[done])
        mine, other = lax.slice_in_dim(total, 0, 1, axis=axis), lax.slice_in_dim(total, 1, 2, axis=axis)
        state[k] = [exchange(other, order[done]), mine, done + 1]
    return jnp.concatenate(outs, axis=1)


def dense(tokens, expert_ids, gate_values, w_gate, w_up, w_down):
    experts = lax.axis_size("expert")
    count, width = tokens.shape
    weights = expert_weights(expert_ids, gate_values, experts)
    high = lax.reduce_precision(weights, 8, 7)
    packed = jnp.concatenate([high, weights - high], axis=1).astype(jnp.bfloat16)
    packed = jnp.pad(packed, ((0, 0), (0, -2 * experts % 128)))
    gates, ups, spread = gather_rows(tokens, packed, w_gate[0], w_up[0], chunks_of(width, GATHER))
    hidden = [(jax.nn.silu(gate) * up).astype(jnp.bfloat16) for gate, up in zip(gates, ups)]
    me = lax.axis_index("expert")
    column = jnp.arange(spread[0].shape[1], dtype=jnp.int32)
    named = (column == me) | (column == me + experts)
    scale = [
        jnp.sum(jnp.where(named[None, :], rows.astype(jnp.float32), 0.0), axis=1, keepdims=True)
        for rows in spread
    ]
    return scatter_rows(hidden, scale, w_down[0], chunks_of(width, SCATTER))


def local(tokens, expert_ids, gate_values, w_gate, w_up, w_down):
    experts = lax.axis_size("expert")
    count, top = expert_ids.shape
    capacity = min(count, max(2, 2 * count * top // experts))
    if capacity < count or experts != 16 or lax.axis_size("tensor") != 2:
        return slotted(tokens, expert_ids, gate_values, w_gate, w_up, w_down, capacity)
    return dense(tokens, expert_ids, gate_values, w_gate, w_up, w_down)


def solution(mesh):
    return jax.shard_map(
        local,
        mesh=mesh,
        in_specs=(
            P(("expert", "tensor"), None),
            P(("expert", "tensor"), None),
            P(("expert", "tensor"), None),
            P("expert", None, "tensor"),
            P("expert", None, "tensor"),
            P("expert", "tensor", None),
        ),
        out_specs=P(("expert", "tensor"), None),
        check_vma=False,
    )
```

```python
import jax
import jax.numpy as jnp
from jax import lax
from jax.sharding import PartitionSpec as P

AXES = ("expert", "tensor")


def slot_places(expert_ids, experts, capacity):
    count = expert_ids.shape[0] * expert_ids.shape[1]
    flat = expert_ids.reshape(count)
    onehot = (flat[:, None] == jnp.arange(experts, dtype=jnp.int32)[None, :]).astype(jnp.int32)
    ranks = jnp.sum(jnp.cumsum(onehot, axis=0) * onehot, axis=1) - 1
    return flat * capacity + ranks


def dispatch_rows(tokens, places, experts, capacity, top):
    count = tokens.shape[0]
    table = (places[:, None] == jnp.arange(experts * capacity, dtype=jnp.int32)[None, :]).astype(
        jnp.bfloat16
    )
    table = jnp.sum(table.reshape(count, top, experts * capacity), axis=1)
    rows = jnp.einsum("ns,nd->sd", table, tokens, preferred_element_type=jnp.float32)
    return rows.astype(jnp.bfloat16).reshape(experts, capacity, tokens.shape[1])


def swiglu(rows, wg, wu):
    gate = jnp.dot(rows, wg, preferred_element_type=jnp.float32)
    up = jnp.dot(rows, wu, preferred_element_type=jnp.float32)
    return (jax.nn.silu(gate) * up).astype(jnp.bfloat16)


def slotted(tokens, expert_ids, gate_values, w_gate, w_up, w_down, capacity):
    experts = lax.axis_size("expert")
    count, top = expert_ids.shape
    width = tokens.shape[1]
    places = slot_places(expert_ids, experts, capacity)
    sending = dispatch_rows(tokens, places, experts, capacity, top)
    arrived = lax.all_to_all(sending, "expert", split_axis=0, concat_axis=0, tiled=True)
    rows = arrived.reshape(experts * capacity, width)
    hidden = swiglu(lax.all_gather(rows, "tensor", axis=0, tiled=True), w_gate[0], w_up[0])
    summed = lax.psum_scatter(
        jnp.dot(hidden, w_down[0], preferred_element_type=jnp.float32).astype(jnp.bfloat16),
        "tensor",
        scatter_dimension=0,
        tiled=True,
    )
    out_rows = summed.reshape(experts, capacity, width)
    returned = lax.all_to_all(out_rows, "expert", split_axis=0, concat_axis=0, tiled=True)
    picked = returned.reshape(experts * capacity, width)[places].reshape(count, top, width)
    mixed = jnp.sum(gate_values[:, :, None] * picked.astype(jnp.float32), axis=1)
    return mixed.astype(jnp.bfloat16)


def expert_weights(expert_ids, gate_values, experts):
    named = expert_ids[:, :, None] == jnp.arange(experts, dtype=jnp.int32)[None, None, :]
    return jnp.sum(jnp.where(named, gate_values[:, :, None], 0.0), axis=1)


def partner(step, e, t):
    if step == "core":
        return e ^ 1, t
    if step in ("far", "near"):
        return (e ^ 4, t) if (e & 1) == (step == "far") else (e ^ 8, t)
    return (e, t ^ 1) if (e & 1) == (step == "late") else (e ^ 2, t)


def exchange(block, step):
    parts = lax.axis_size("tensor")
    perm = []
    for e in range(lax.axis_size("expert")):
        for t in range(parts):
            other = partner(step, e, t)
            perm.append((e * parts + t, other[0] * parts + other[1]))
    return lax.ppermute(block, AXES, perm)


STEPS = ("far", "near", "late", "early")
GATHER = (
    (22, ("near", "far", "early", "late")),
    (16, ("near", "early", "far", "late")),
    (18, ("far", "early", "late", "near")),
)
SCATTER = (
    (19, ("late", "early", "far", "near")),
    (18, ("near", "late", "early", "far")),
    (19, ("late", "early", "near", "far")),
)
GATHER_TURNS = (10, 1, 12, 10, 11, 2, 10, 11, 12, 10, 12, 11, 10, 10, 10, 12, 11, 11, 12, 11, 12)
SCATTER_TURNS = (0, 11, 2, 0, 2, 0, 1, 2, 0, 1, 2, 0, 1, 2, 11)
PACKED = 2


def chunks_of(width, plan):
    tiles, total = width // 128, sum(share for share, _ in plan)
    edges, at = [0], 0
    for share, _ in plan:
        at += share
        edges.append(128 * (tiles * at // total))
    return [(lo, hi, order) for lo, hi, (_, order) in zip(edges[:-1], edges[1:], plan)]


def gather_rows(tokens, packed, w_gate, w_up, chunks):
    count, width = tokens.shape
    blocks = [tokens[:, lo:hi] for lo, hi, _ in chunks]
    blocks[PACKED] = jnp.concatenate([blocks[PACKED], packed], axis=1)
    state = [[block.reshape(1, 1, 1, 1, count, -1), None, 0] for block in blocks]
    before = tokens
    gates, ups, spread = [0.0, 0.0], [0.0, 0.0], [None, None]

    def products(k, j, rows):
        lo, hi, _ = chunks[k]
        if k == PACKED:
            spread[j], rows = rows[:, hi - lo :], rows[:, : hi - lo]
        gates[j] = gates[j] + jnp.dot(rows, w_gate[lo:hi], preferred_element_type=jnp.float32)
        ups[j] = ups[j] + jnp.dot(rows, w_up[lo:hi], preferred_element_type=jnp.float32)
        return ups[j]

    for k in GATHER_TURNS:
        free, k = k >= 10, k % 10
        rows, arrived, done = state[k]
        order = chunks[k][2]
        if free:
            pass
        elif done > 0 and done != len(order) + 1:
            arrived, before = lax.optimization_barrier((arrived, before))
        elif done > 0:
            rows, before = lax.optimization_barrier((rows, before))
        if 0 < done <= len(order):
            rows = jnp.concatenate([rows, arrived], axis=STEPS.index(order[done - 1]))
            before = rows
        if done < len(order):
            arrived = exchange(rows, order[done])
        elif done == len(order):
            rows = rows.reshape(16 * count, -1)
            arrived = exchange(rows, "core")
        elif done == len(order) + 1:
            before = products(k, 0, rows)
        else:
            before = products(k, 1, arrived)
        state[k] = [rows, arrived, done + 1]
    return gates, ups, spread


def scatter_rows(hidden, scale, w_down, chunks):
    def product(j, chunk):
        lo, hi, _ = chunk
        return scale[j] * jnp.dot(hidden[j], w_down[:, lo:hi], preferred_element_type=jnp.float32)

    state = [[exchange(product(1, chunk).astype(jnp.bfloat16), "core"), None, 0] for chunk in chunks]
    before = hidden[0]
    count = hidden[0].shape[0] // 16
    outs = [None] * len(chunks)
    for k in SCATTER_TURNS:
        free, k = k >= 10, k % 10
        arrived, mine, done = state[k]
        lo, hi, order = chunks[k]
        if not free:
            arrived, before = lax.optimization_barrier((arrived, before))
        if done == 0:
            total = product(0, chunks[k]) + arrived.astype(jnp.float32)
            total = total.reshape(2, 2, 2, 2, count, hi - lo).astype(jnp.bfloat16)
        else:
            total = (mine.astype(jnp.float32) + arrived.astype(jnp.float32)).astype(jnp.bfloat16)
        before = total
        if done == len(order):
            outs[k] = total.reshape(count, hi - lo)
            continue
        axis = STEPS.index(order[done])
        mine, other = lax.slice_in_dim(total, 0, 1, axis=axis), lax.slice_in_dim(total, 1, 2, axis=axis)
        state[k] = [exchange(other, order[done]), mine, done + 1]
    return jnp.concatenate(outs, axis=1)


def dense(tokens, expert_ids, gate_values, w_gate, w_up, w_down):
    experts = lax.axis_size("expert")
    count, width = tokens.shape
    weights = expert_weights(expert_ids, gate_values, experts)
    high = lax.reduce_precision(weights, 8, 7)
    packed = jnp.concatenate([high, weights - high], axis=1).astype(jnp.bfloat16)
    packed = jnp.pad(packed, ((0, 0), (0, -2 * experts % 128)))
    gates, ups, spread = gather_rows(tokens, packed, w_gate[0], w_up[0], chunks_of(width, GATHER))
    hidden = [(jax.nn.silu(gate) * up).astype(jnp.bfloat16) for gate, up in zip(gates, ups)]
    me = lax.axis_index("expert")
    column = jnp.arange(spread[0].shape[1], dtype=jnp.int32)
    named = (column == me) | (column == me + experts)
    scale = [
        jnp.sum(jnp.where(named[None, :], rows.astype(jnp.float32), 0.0), axis=1, keepdims=True)
        for rows in spread
    ]
    return scatter_rows(hidden, scale, w_down[0], chunks_of(width, SCATTER))


def local(tokens, expert_ids, gate_values, w_gate, w_up, w_down):
    experts = lax.axis_size("expert")
    count, top = expert_ids.shape
    capacity = min(count, max(2, 2 * count * top // experts))
    if capacity < count or experts != 16 or lax.axis_size("tensor") != 2:
        return slotted(tokens, expert_ids, gate_values, w_gate, w_up, w_down, capacity)
    return dense(tokens, expert_ids, gate_values, w_gate, w_up, w_down)


def solution(mesh):
    return jax.shard_map(
        local,
        mesh=mesh,
        in_specs=(
            P(("expert", "tensor"), None),
            P(("expert", "tensor"), None),
            P(("expert", "tensor"), None),
            P("expert", None, "tensor"),
            P("expert", None, "tensor"),
            P("expert", "tensor", None),
        ),
        out_specs=P(("expert", "tensor"), None),
        check_vma=False,
    )
```

```python
import jax
import jax.numpy as jnp
from jax import lax
from jax.sharding import PartitionSpec as P

AXES = ("expert", "tensor")


def slot_places(expert_ids, experts, capacity):
    count = expert_ids.shape[0] * expert_ids.shape[1]
    flat = expert_ids.reshape(count)
    onehot = (flat[:, None] == jnp.arange(experts, dtype=jnp.int32)[None, :]).astype(jnp.int32)
    ranks = jnp.sum(jnp.cumsum(onehot, axis=0) * onehot, axis=1) - 1
    return flat * capacity + ranks


def dispatch_rows(tokens, places, experts, capacity, top):
    count = tokens.shape[0]
    table = (places[:, None] == jnp.arange(experts * capacity, dtype=jnp.int32)[None, :]).astype(
        jnp.bfloat16
    )
    table = jnp.sum(table.reshape(count, top, experts * capacity), axis=1)
    rows = jnp.einsum("ns,nd->sd", table, tokens, preferred_element_type=jnp.float32)
    return rows.astype(jnp.bfloat16).reshape(experts, capacity, tokens.shape[1])


def swiglu(rows, wg, wu):
    gate = jnp.dot(rows, wg, preferred_element_type=jnp.float32)
    up = jnp.dot(rows, wu, preferred_element_type=jnp.float32)
    return (jax.nn.silu(gate) * up).astype(jnp.bfloat16)


def slotted(tokens, expert_ids, gate_values, w_gate, w_up, w_down, capacity):
    experts = lax.axis_size("expert")
    count, top = expert_ids.shape
    width = tokens.shape[1]
    places = slot_places(expert_ids, experts, capacity)
    sending = dispatch_rows(tokens, places, experts, capacity, top)
    arrived = lax.all_to_all(sending, "expert", split_axis=0, concat_axis=0, tiled=True)
    rows = arrived.reshape(experts * capacity, width)
    hidden = swiglu(lax.all_gather(rows, "tensor", axis=0, tiled=True), w_gate[0], w_up[0])
    summed = lax.psum_scatter(
        jnp.dot(hidden, w_down[0], preferred_element_type=jnp.float32).astype(jnp.bfloat16),
        "tensor",
        scatter_dimension=0,
        tiled=True,
    )
    out_rows = summed.reshape(experts, capacity, width)
    returned = lax.all_to_all(out_rows, "expert", split_axis=0, concat_axis=0, tiled=True)
    picked = returned.reshape(experts * capacity, width)[places].reshape(count, top, width)
    mixed = jnp.sum(gate_values[:, :, None] * picked.astype(jnp.float32), axis=1)
    return mixed.astype(jnp.bfloat16)


def expert_weights(expert_ids, gate_values, experts):
    named = expert_ids[:, :, None] == jnp.arange(experts, dtype=jnp.int32)[None, None, :]
    return jnp.sum(jnp.where(named, gate_values[:, :, None], 0.0), axis=1)


def partner(step, e, t):
    if step == "core":
        return e ^ 1, t
    if step == "far":
        return e ^ 8, t
    if step == "near":
        return e ^ 4, t
    return (e, t ^ 1) if (e & 1) == (step == "late") else (e ^ 2, t)


def exchange(block, step):
    parts = lax.axis_size("tensor")
    perm = []
    for e in range(lax.axis_size("expert")):
        for t in range(parts):
            other = partner(step, e, t)
            perm.append((e * parts + t, other[0] * parts + other[1]))
    return lax.ppermute(block, AXES, perm)


STEPS = ("far", "near", "late", "early")
GATHER = (
    (20, ("far", "early", "late", "near")),
    (24, ("far", "near", "early", "late")),
    (12, ("far", "near", "early", "late")),
)
SCATTER = (
    (19, ("late", "early", "near", "far")),
    (20, ("near", "late", "early", "far")),
    (17, ("late", "early", "near", "far")),
)
GATHER_TURNS = (10, 11, 12, 10, 12, 11, 10, 12, 11, 10, 12, 11, 12, 12, 12, 10, 10, 11, 11, 11, 10)
SCATTER_TURNS = (0, 1, 2, 0, 2, 0, 1, 2, 0, 1, 2, 1, 0, 2, 1)
PACKED = 1


def chunks_of(width, plan):
    tiles, total = width // 128, sum(share for share, _ in plan)
    edges, at = [0], 0
    for share, _ in plan:
        at += share
        edges.append(128 * (tiles * at // total))
    return [(lo, hi, order) for lo, hi, (_, order) in zip(edges[:-1], edges[1:], plan)]


def gather_rows(tokens, packed, w_gate, w_up, chunks):
    count, width = tokens.shape
    blocks = [tokens[:, lo:hi] for lo, hi, _ in chunks]
    blocks[PACKED] = jnp.concatenate([blocks[PACKED], packed], axis=1)
    state = [[block.reshape(1, 1, 1, 1, count, -1), None, 0] for block in blocks]
    before = tokens
    gates, ups, spread = [0.0, 0.0], [0.0, 0.0], [None, None]

    def products(k, j, rows):
        lo, hi, _ = chunks[k]
        if k == PACKED:
            spread[j], rows = rows[:, hi - lo :], rows[:, : hi - lo]
        gates[j] = gates[j] + jnp.dot(rows, w_gate[lo:hi], preferred_element_type=jnp.float32)
        ups[j] = ups[j] + jnp.dot(rows, w_up[lo:hi], preferred_element_type=jnp.float32)
        return ups[j]

    for k in GATHER_TURNS:
        free, k = k >= 10, k % 10
        rows, arrived, done = state[k]
        order = chunks[k][2]
        if free:
            pass
        elif done > 0 and done != len(order) + 1:
            arrived, before = lax.optimization_barrier((arrived, before))
        elif done > 0:
            rows, before = lax.optimization_barrier((rows, before))
        if 0 < done <= len(order):
            rows = jnp.concatenate([rows, arrived], axis=STEPS.index(order[done - 1]))
            before = rows
        if done < len(order):
            arrived = exchange(rows, order[done])
        elif done == len(order):
            rows = rows.reshape(16 * count, -1)
            arrived = exchange(rows, "core")
        elif done == len(order) + 1:
            before = products(k, 0, rows)
        else:
            before = products(k, 1, arrived)
        state[k] = [rows, arrived, done + 1]
    return gates, ups, spread


def scatter_rows(hidden, scale, w_down, chunks):
    def product(j, chunk):
        lo, hi, _ = chunk
        return scale[j] * jnp.dot(hidden[j], w_down[:, lo:hi], preferred_element_type=jnp.float32)

    state = [[exchange(product(1, chunk).astype(jnp.bfloat16), "core"), None, 0] for chunk in chunks]
    before = hidden[0]
    count = hidden[0].shape[0] // 16
    outs = [None] * len(chunks)
    for k in SCATTER_TURNS:
        free, k = k >= 10, k % 10
        arrived, mine, done = state[k]
        lo, hi, order = chunks[k]
        if not free:
            arrived, before = lax.optimization_barrier((arrived, before))
        if done == 0:
            total = product(0, chunks[k]) + arrived.astype(jnp.float32)
            total = total.reshape(2, 2, 2, 2, count, hi - lo).astype(jnp.bfloat16)
        else:
            total = (mine.astype(jnp.float32) + arrived.astype(jnp.float32)).astype(jnp.bfloat16)
        before = total
        if done == len(order):
            outs[k] = total.reshape(count, hi - lo)
            continue
        axis = STEPS.index(order[done])
        mine, other = lax.slice_in_dim(total, 0, 1, axis=axis), lax.slice_in_dim(total, 1, 2, axis=axis)
        state[k] = [exchange(other, order[done]), mine, done + 1]
    return jnp.concatenate(outs, axis=1)


def dense(tokens, expert_ids, gate_values, w_gate, w_up, w_down):
    experts = lax.axis_size("expert")
    count, width = tokens.shape
    weights = expert_weights(expert_ids, gate_values, experts)
    high = lax.reduce_precision(weights, 8, 7)
    packed = jnp.concatenate([high, weights - high], axis=1).astype(jnp.bfloat16)
    packed = jnp.pad(packed, ((0, 0), (0, -2 * experts % 128)))
    gates, ups, spread = gather_rows(tokens, packed, w_gate[0], w_up[0], chunks_of(width, GATHER))
    hidden = [(jax.nn.silu(gate) * up).astype(jnp.bfloat16) for gate, up in zip(gates, ups)]
    me = lax.axis_index("expert")
    column = jnp.arange(spread[0].shape[1], dtype=jnp.int32)
    named = (column == me) | (column == me + experts)
    scale = [
        jnp.sum(jnp.where(named[None, :], rows.astype(jnp.float32), 0.0), axis=1, keepdims=True)
        for rows in spread
    ]
    return scatter_rows(hidden, scale, w_down[0], chunks_of(width, SCATTER))


def local(tokens, expert_ids, gate_values, w_gate, w_up, w_down):
    experts = lax.axis_size("expert")
    count, top = expert_ids.shape
    capacity = min(count, max(2, 2 * count * top // experts))
    if capacity < count or experts != 16 or lax.axis_size("tensor") != 2:
        return slotted(tokens, expert_ids, gate_values, w_gate, w_up, w_down, capacity)
    return dense(tokens, expert_ids, gate_values, w_gate, w_up, w_down)


def solution(mesh):
    return jax.shard_map(
        local,
        mesh=mesh,
        in_specs=(
            P(("expert", "tensor"), None),
            P(("expert", "tensor"), None),
            P(("expert", "tensor"), None),
            P("expert", None, "tensor"),
            P("expert", None, "tensor"),
            P("expert", "tensor", None),
        ),
        out_specs=P(("expert", "tensor"), None),
        check_vma=False,
    )
```

```python
import jax
import jax.numpy as jnp
from jax import lax
from jax.sharding import PartitionSpec as P

AXES = ("expert", "tensor")


def slot_places(expert_ids, experts, capacity):
    count = expert_ids.shape[0] * expert_ids.shape[1]
    flat = expert_ids.reshape(count)
    onehot = (flat[:, None] == jnp.arange(experts, dtype=jnp.int32)[None, :]).astype(jnp.int32)
    ranks = jnp.sum(jnp.cumsum(onehot, axis=0) * onehot, axis=1) - 1
    return flat * capacity + ranks


def dispatch_rows(tokens, places, experts, capacity, top):
    count = tokens.shape[0]
    table = (places[:, None] == jnp.arange(experts * capacity, dtype=jnp.int32)[None, :]).astype(
        jnp.bfloat16
    )
    table = jnp.sum(table.reshape(count, top, experts * capacity), axis=1)
    rows = jnp.einsum("ns,nd->sd", table, tokens, preferred_element_type=jnp.float32)
    return rows.astype(jnp.bfloat16).reshape(experts, capacity, tokens.shape[1])


def swiglu(rows, wg, wu):
    gate = jnp.dot(rows, wg, preferred_element_type=jnp.float32)
    up = jnp.dot(rows, wu, preferred_element_type=jnp.float32)
    return (jax.nn.silu(gate) * up).astype(jnp.bfloat16)


def slotted(tokens, expert_ids, gate_values, w_gate, w_up, w_down, capacity):
    experts = lax.axis_size("expert")
    count, top = expert_ids.shape
    width = tokens.shape[1]
    places = slot_places(expert_ids, experts, capacity)
    sending = dispatch_rows(tokens, places, experts, capacity, top)
    arrived = lax.all_to_all(sending, "expert", split_axis=0, concat_axis=0, tiled=True)
    rows = arrived.reshape(experts * capacity, width)
    hidden = swiglu(lax.all_gather(rows, "tensor", axis=0, tiled=True), w_gate[0], w_up[0])
    summed = lax.psum_scatter(
        jnp.dot(hidden, w_down[0], preferred_element_type=jnp.float32).astype(jnp.bfloat16),
        "tensor",
        scatter_dimension=0,
        tiled=True,
    )
    out_rows = summed.reshape(experts, capacity, width)
    returned = lax.all_to_all(out_rows, "expert", split_axis=0, concat_axis=0, tiled=True)
    picked = returned.reshape(experts * capacity, width)[places].reshape(count, top, width)
    mixed = jnp.sum(gate_values[:, :, None] * picked.astype(jnp.float32), axis=1)
    return mixed.astype(jnp.bfloat16)


def expert_weights(expert_ids, gate_values, experts):
    named = expert_ids[:, :, None] == jnp.arange(experts, dtype=jnp.int32)[None, None, :]
    return jnp.sum(jnp.where(named, gate_values[:, :, None], 0.0), axis=1)


def partner(step, e, t, turned):
    if step == "core":
        return e ^ 1, t
    if step in ("far", "near"):
        return (e ^ 8, t) if (step == "far") != (turned and e & 1 == 1) else (e ^ 4, t)
    return (e, t ^ 1) if (e & 1) == (step == "late") else (e ^ 2, t)


def exchange(block, step, turned=False):
    parts = lax.axis_size("tensor")
    perm = []
    for e in range(lax.axis_size("expert")):
        for t in range(parts):
            other = partner(step, e, t, turned)
            perm.append((e * parts + t, other[0] * parts + other[1]))
    return lax.ppermute(block, AXES, perm)


STEPS = ("far", "near", "late", "early")
GATHER = (
    (20, ("far", "early", "late", "near")),
    (24, ("far", "near", "early", "late")),
    (12, ("far", "near", "early", "late")),
)
SCATTER = (
    (19, ("late", "early", "far", "near")),
    (18, ("near", "late", "early", "far")),
    (19, ("late", "early", "near", "far")),
)
GATHER_TURNS = (10, 11, 12, 10, 12, 11, 10, 12, 11, 10, 12, 11, 12, 10, 12, 12, 1, 10, 11, 11, 10)
SCATTER_TURNS = (0, 11, 2, 0, 2, 0, 1, 2, 0, 1, 2, 0, 1, 2, 11)
PACKED = 1


def chunks_of(width, plan):
    tiles, total = width // 128, sum(share for share, _ in plan)
    edges, at = [0], 0
    for share, _ in plan:
        at += share
        edges.append(128 * (tiles * at // total))
    return [(lo, hi, order) for lo, hi, (_, order) in zip(edges[:-1], edges[1:], plan)]


def gather_rows(tokens, packed, w_gate, w_up, chunks):
    count, width = tokens.shape
    blocks = [tokens[:, lo:hi] for lo, hi, _ in chunks]
    blocks[PACKED] = jnp.concatenate([blocks[PACKED], packed], axis=1)
    state = [[block.reshape(1, 1, 1, 1, count, -1), None, 0] for block in blocks]
    before = tokens
    gates, ups, spread = [0.0, 0.0], [0.0, 0.0], [None, None]

    def products(k, j, rows):
        lo, hi, _ = chunks[k]
        if k == PACKED:
            spread[j], rows = rows[:, hi - lo :], rows[:, : hi - lo]
        gates[j] = gates[j] + jnp.dot(rows, w_gate[lo:hi], preferred_element_type=jnp.float32)
        ups[j] = ups[j] + jnp.dot(rows, w_up[lo:hi], preferred_element_type=jnp.float32)
        return gates[j], ups[j]

    for k in GATHER_TURNS:
        free, k = k >= 10, k % 10
        rows, arrived, done = state[k]
        order = chunks[k][2]
        if free:
            pass
        elif done > 0 and done != len(order) + 1:
            arrived, before = lax.optimization_barrier((arrived, before))
        elif done > 0:
            rows, before = lax.optimization_barrier((rows, before))
        if 0 < done <= len(order):
            rows = jnp.concatenate([rows, arrived], axis=STEPS.index(order[done - 1]))
            before = rows
        if done < len(order):
            arrived = exchange(rows, order[done])
        elif done == len(order):
            rows = rows.reshape(16 * count, -1)
            arrived = exchange(rows, "core")
        elif done == len(order) + 1:
            before = products(k, 0, rows)
        else:
            before = products(k, 1, arrived)
        state[k] = [rows, arrived, done + 1]
    return gates, ups, spread


def scatter_rows(hidden, scale, w_down, chunks):
    core = lax.axis_index("expert") & 1

    def turn(rows, j):
        turned = rows.reshape(2, 2, -1, rows.shape[1]).swapaxes(0, 1).reshape(rows.shape)
        return jnp.where(core != j, turned, rows)

    hidden = [turn(rows, j) for j, rows in enumerate(hidden)]
    scale = [turn(rows, j) for j, rows in enumerate(scale)]

    def product(j, chunk):
        lo, hi, _ = chunk
        return scale[j] * jnp.dot(hidden[j], w_down[:, lo:hi], preferred_element_type=jnp.float32)

    state = [[exchange(product(1, chunk).astype(jnp.bfloat16), "core"), None, 0] for chunk in chunks]
    before = hidden[0]
    count = hidden[0].shape[0] // 16
    outs = [None] * len(chunks)
    for k in SCATTER_TURNS:
        free, k = k >= 10, k % 10
        arrived, mine, done = state[k]
        lo, hi, order = chunks[k]
        if not free:
            arrived, before = lax.optimization_barrier((arrived, before))
        if done == 0:
            total = product(0, chunks[k]) + arrived.astype(jnp.float32)
            total = total.reshape(2, 2, 2, 2, count, hi - lo).astype(jnp.bfloat16)
        else:
            total = (mine.astype(jnp.float32) + arrived.astype(jnp.float32)).astype(jnp.bfloat16)
        before = total
        if done == len(order):
            outs[k] = total.reshape(count, hi - lo)
            continue
        axis = STEPS.index(order[done])
        mine, other = lax.slice_in_dim(total, 0, 1, axis=axis), lax.slice_in_dim(total, 1, 2, axis=axis)
        state[k] = [exchange(other, order[done], True), mine, done + 1]
    return jnp.concatenate(outs, axis=1)


def dense(tokens, expert_ids, gate_values, w_gate, w_up, w_down):
    experts = lax.axis_size("expert")
    count, width = tokens.shape
    weights = expert_weights(expert_ids, gate_values, experts)
    high = lax.reduce_precision(weights, 8, 7)
    packed = jnp.concatenate([high, weights - high], axis=1).astype(jnp.bfloat16)
    packed = jnp.pad(packed, ((0, 0), (0, -2 * experts % 128)))
    gates, ups, spread = gather_rows(tokens, packed, w_gate[0], w_up[0], chunks_of(width, GATHER))
    hidden = [(jax.nn.silu(gate) * up).astype(jnp.bfloat16) for gate, up in zip(gates, ups)]
    me = lax.axis_index("expert")
    column = jnp.arange(spread[0].shape[1], dtype=jnp.int32)
    named = (column == me) | (column == me + experts)
    scale = [
        jnp.sum(jnp.where(named[None, :], rows.astype(jnp.float32), 0.0), axis=1, keepdims=True)
        for rows in spread
    ]
    return scatter_rows(hidden, scale, w_down[0], chunks_of(width, SCATTER))


def local(tokens, expert_ids, gate_values, w_gate, w_up, w_down):
    experts = lax.axis_size("expert")
    count, top = expert_ids.shape
    capacity = min(count, max(2, 2 * count * top // experts))
    if capacity < count or experts != 16 or lax.axis_size("tensor") != 2:
        return slotted(tokens, expert_ids, gate_values, w_gate, w_up, w_down, capacity)
    return dense(tokens, expert_ids, gate_values, w_gate, w_up, w_down)


def solution(mesh):
    return jax.shard_map(
        local,
        mesh=mesh,
        in_specs=(
            P(("expert", "tensor"), None),
            P(("expert", "tensor"), None),
            P(("expert", "tensor"), None),
            P("expert", None, "tensor"),
            P("expert", None, "tensor"),
            P("expert", "tensor", None),
        ),
        out_specs=P(("expert", "tensor"), None),
        check_vma=False,
    )
```

```python
import jax
import jax.numpy as jnp
from jax import lax
from jax.sharding import PartitionSpec as P

AXES = ("expert", "tensor")


def slot_places(expert_ids, experts, capacity):
    count = expert_ids.shape[0] * expert_ids.shape[1]
    flat = expert_ids.reshape(count)
    onehot = (flat[:, None] == jnp.arange(experts, dtype=jnp.int32)[None, :]).astype(jnp.int32)
    ranks = jnp.sum(jnp.cumsum(onehot, axis=0) * onehot, axis=1) - 1
    return flat * capacity + ranks


def dispatch_rows(tokens, places, experts, capacity, top):
    count = tokens.shape[0]
    table = (places[:, None] == jnp.arange(experts * capacity, dtype=jnp.int32)[None, :]).astype(
        jnp.bfloat16
    )
    table = jnp.sum(table.reshape(count, top, experts * capacity), axis=1)
    rows = jnp.einsum("ns,nd->sd", table, tokens, preferred_element_type=jnp.float32)
    return rows.astype(jnp.bfloat16).reshape(experts, capacity, tokens.shape[1])


def swiglu(rows, wg, wu):
    gate = jnp.dot(rows, wg, preferred_element_type=jnp.float32)
    up = jnp.dot(rows, wu, preferred_element_type=jnp.float32)
    return (jax.nn.silu(gate) * up).astype(jnp.bfloat16)


def slotted(tokens, expert_ids, gate_values, w_gate, w_up, w_down, capacity):
    experts = lax.axis_size("expert")
    count, top = expert_ids.shape
    width = tokens.shape[1]
    places = slot_places(expert_ids, experts, capacity)
    sending = dispatch_rows(tokens, places, experts, capacity, top)
    arrived = lax.all_to_all(sending, "expert", split_axis=0, concat_axis=0, tiled=True)
    rows = arrived.reshape(experts * capacity, width)
    hidden = swiglu(lax.all_gather(rows, "tensor", axis=0, tiled=True), w_gate[0], w_up[0])
    summed = lax.psum_scatter(
        jnp.dot(hidden, w_down[0], preferred_element_type=jnp.float32).astype(jnp.bfloat16),
        "tensor",
        scatter_dimension=0,
        tiled=True,
    )
    out_rows = summed.reshape(experts, capacity, width)
    returned = lax.all_to_all(out_rows, "expert", split_axis=0, concat_axis=0, tiled=True)
    picked = returned.reshape(experts * capacity, width)[places].reshape(count, top, width)
    mixed = jnp.sum(gate_values[:, :, None] * picked.astype(jnp.float32), axis=1)
    return mixed.astype(jnp.bfloat16)


def expert_weights(expert_ids, gate_values, experts):
    named = expert_ids[:, :, None] == jnp.arange(experts, dtype=jnp.int32)[None, None, :]
    return jnp.sum(jnp.where(named, gate_values[:, :, None], 0.0), axis=1)


def partner(step, e, t, turned):
    if step == "core":
        return e ^ 1, t
    if step in ("far", "near"):
        return (e ^ 8, t) if (step == "far") != (turned and e & 1 == 1) else (e ^ 4, t)
    return (e, t ^ 1) if (e & 1) == (step == "late") else (e ^ 2, t)


def exchange(block, step, turned=False):
    parts = lax.axis_size("tensor")
    perm = []
    for e in range(lax.axis_size("expert")):
        for t in range(parts):
            other = partner(step, e, t, turned)
            perm.append((e * parts + t, other[0] * parts + other[1]))
    return lax.ppermute(block, AXES, perm)


STEPS = ("far", "near", "late", "early")
GATHER = (
    (20, ("far", "early", "late", "near")),
    (24, ("far", "near", "early", "late")),
    (12, ("far", "near", "early", "late")),
)
SCATTER = (
    (19, ("late", "early", "far", "near")),
    (18, ("near", "late", "early", "far")),
    (19, ("late", "early", "near", "far")),
)
GATHER_TURNS = (10, 11, 12, 10, 12, 11, 10, 12, 11, 10, 12, 11, 12, 12, 12, 10, 10, 11, 11, 11, 10)
SCATTER_TURNS = (0, 11, 12, 0, 2, 10, 1, 2, 10, 1, 0, 2, 1, 2, 11)
PACKED = 1


def chunks_of(width, plan):
    tiles, total = width // 128, sum(share for share, _ in plan)
    edges, at = [0], 0
    for share, _ in plan:
        at += share
        edges.append(128 * (tiles * at // total))
    return [(lo, hi, order) for lo, hi, (_, order) in zip(edges[:-1], edges[1:], plan)]


def gather_rows(tokens, packed, w_gate, w_up, chunks):
    count, width = tokens.shape
    blocks = [tokens[:, lo:hi] for lo, hi, _ in chunks]
    blocks[PACKED] = jnp.concatenate([blocks[PACKED], packed], axis=1)
    state = [[block.reshape(1, 1, 1, 1, count, -1), None, 0] for block in blocks]
    before = tokens
    gates, ups, spread = [0.0, 0.0], [0.0, 0.0], [None, None]

    def products(k, j, rows):
        lo, hi, _ = chunks[k]
        if k == PACKED:
            spread[j], rows = rows[:, hi - lo :], rows[:, : hi - lo]
        gates[j] = gates[j] + jnp.dot(rows, w_gate[lo:hi], preferred_element_type=jnp.float32)
        ups[j] = ups[j] + jnp.dot(rows, w_up[lo:hi], preferred_element_type=jnp.float32)
        return gates[j], ups[j]

    for k in GATHER_TURNS:
        free, k = k >= 10, k % 10
        rows, arrived, done = state[k]
        order = chunks[k][2]
        if free:
            pass
        elif done > 0 and done != len(order) + 1:
            arrived, before = lax.optimization_barrier((arrived, before))
        elif done > 0:
            rows, before = lax.optimization_barrier((rows, before))
        if 0 < done <= len(order):
            rows = jnp.concatenate([rows, arrived], axis=STEPS.index(order[done - 1]))
            before = rows
        if done < len(order):
            arrived = exchange(rows, order[done])
        elif done == len(order):
            rows = rows.reshape(16 * count, -1)
            arrived = exchange(rows, "core")
        elif done == len(order) + 1:
            before = products(k, 0, rows)
        else:
            before = products(k, 1, arrived)
        state[k] = [rows, arrived, done + 1]
    return gates, ups, spread


def scatter_rows(hidden, w_down, chunks):
    core = lax.axis_index("expert") & 1

    def turn(rows, j):
        turned = rows.reshape(2, 2, -1, rows.shape[1]).swapaxes(0, 1).reshape(rows.shape)
        return jnp.where(core != j, turned, rows)

    hidden = [turn(rows, j) for j, rows in enumerate(hidden)]

    def product(j, chunk):
        lo, hi, _ = chunk
        return jnp.dot(hidden[j], w_down[:, lo:hi], preferred_element_type=jnp.float32)

    state = [[exchange(product(1, chunk).astype(jnp.bfloat16), "core"), None, 0] for chunk in chunks]
    before = hidden[0]
    count = hidden[0].shape[0] // 16
    outs = [None] * len(chunks)
    for k in SCATTER_TURNS:
        free, k = k >= 10, k % 10
        arrived, mine, done = state[k]
        lo, hi, order = chunks[k]
        if not free:
            arrived, before = lax.optimization_barrier((arrived, before))
        if done == 0:
            total = product(0, chunks[k]) + arrived.astype(jnp.float32)
            total = total.reshape(2, 2, 2, 2, count, hi - lo).astype(jnp.bfloat16)
        else:
            total = (mine.astype(jnp.float32) + arrived.astype(jnp.float32)).astype(jnp.bfloat16)
        before = total
        if done == len(order):
            outs[k] = total.reshape(count, hi - lo)
            continue
        axis = STEPS.index(order[done])
        mine, other = lax.slice_in_dim(total, 0, 1, axis=axis), lax.slice_in_dim(total, 1, 2, axis=axis)
        state[k] = [exchange(other, order[done], True), mine, done + 1]
    return jnp.concatenate(outs, axis=1)


def dense(tokens, expert_ids, gate_values, w_gate, w_up, w_down):
    experts = lax.axis_size("expert")
    count, width = tokens.shape
    weights = expert_weights(expert_ids, gate_values, experts)
    high = lax.reduce_precision(weights, 8, 7)
    packed = jnp.concatenate([high, weights - high], axis=1).astype(jnp.bfloat16)
    packed = jnp.pad(packed, ((0, 0), (0, -2 * experts % 128)))
    gates, ups, spread = gather_rows(tokens, packed, w_gate[0], w_up[0], chunks_of(width, GATHER))
    me = lax.axis_index("expert")
    column = jnp.arange(spread[0].shape[1], dtype=jnp.int32)
    named = (column == me) | (column == me + experts)
    hidden = []
    for gate, up, rows in zip(gates, ups, spread):
        scale = jnp.sum(jnp.where(named[None, :], rows.astype(jnp.float32), 0.0), axis=1, keepdims=True)
        hidden.append((scale * (jax.nn.silu(gate) * up)).astype(jnp.bfloat16))
    return scatter_rows(hidden, w_down[0], chunks_of(width, SCATTER))


def local(tokens, expert_ids, gate_values, w_gate, w_up, w_down):
    experts = lax.axis_size("expert")
    count, top = expert_ids.shape
    capacity = min(count, max(2, 2 * count * top // experts))
    if capacity < count or experts != 16 or lax.axis_size("tensor") != 2:
        return slotted(tokens, expert_ids, gate_values, w_gate, w_up, w_down, capacity)
    return dense(tokens, expert_ids, gate_values, w_gate, w_up, w_down)


def solution(mesh):
    return jax.shard_map(
        local,
        mesh=mesh,
        in_specs=(
            P(("expert", "tensor"), None),
            P(("expert", "tensor"), None),
            P(("expert", "tensor"), None),
            P("expert", None, "tensor"),
            P("expert", None, "tensor"),
            P("expert", "tensor", None),
        ),
        out_specs=P(("expert", "tensor"), None),
        check_vma=False,
    )
```

```python
import jax
import jax.numpy as jnp
from jax import lax
from jax.sharding import PartitionSpec as P

AXES = ("expert", "tensor")


def slot_places(expert_ids, experts, capacity):
    count = expert_ids.shape[0] * expert_ids.shape[1]
    flat = expert_ids.reshape(count)
    onehot = (flat[:, None] == jnp.arange(experts, dtype=jnp.int32)[None, :]).astype(jnp.int32)
    ranks = jnp.sum(jnp.cumsum(onehot, axis=0) * onehot, axis=1) - 1
    return flat * capacity + ranks


def dispatch_rows(tokens, places, experts, capacity, top):
    count = tokens.shape[0]
    table = (places[:, None] == jnp.arange(experts * capacity, dtype=jnp.int32)[None, :]).astype(
        jnp.bfloat16
    )
    table = jnp.sum(table.reshape(count, top, experts * capacity), axis=1)
    rows = jnp.einsum("ns,nd->sd", table, tokens, preferred_element_type=jnp.float32)
    return rows.astype(jnp.bfloat16).reshape(experts, capacity, tokens.shape[1])


def swiglu(rows, wg, wu):
    gate = jnp.dot(rows, wg, preferred_element_type=jnp.float32)
    up = jnp.dot(rows, wu, preferred_element_type=jnp.float32)
    return (jax.nn.silu(gate) * up).astype(jnp.bfloat16)


def slotted(tokens, expert_ids, gate_values, w_gate, w_up, w_down, capacity):
    experts = lax.axis_size("expert")
    count, top = expert_ids.shape
    width = tokens.shape[1]
    places = slot_places(expert_ids, experts, capacity)
    sending = dispatch_rows(tokens, places, experts, capacity, top)
    arrived = lax.all_to_all(sending, "expert", split_axis=0, concat_axis=0, tiled=True)
    rows = arrived.reshape(experts * capacity, width)
    hidden = swiglu(lax.all_gather(rows, "tensor", axis=0, tiled=True), w_gate[0], w_up[0])
    summed = lax.psum_scatter(
        jnp.dot(hidden, w_down[0], preferred_element_type=jnp.float32).astype(jnp.bfloat16),
        "tensor",
        scatter_dimension=0,
        tiled=True,
    )
    out_rows = summed.reshape(experts, capacity, width)
    returned = lax.all_to_all(out_rows, "expert", split_axis=0, concat_axis=0, tiled=True)
    picked = returned.reshape(experts * capacity, width)[places].reshape(count, top, width)
    mixed = jnp.sum(gate_values[:, :, None] * picked.astype(jnp.float32), axis=1)
    return mixed.astype(jnp.bfloat16)


def expert_weights(expert_ids, gate_values, experts):
    named = expert_ids[:, :, None] == jnp.arange(experts, dtype=jnp.int32)[None, None, :]
    return jnp.sum(jnp.where(named, gate_values[:, :, None], 0.0), axis=1)


def partner(step, e, t):
    if step == "core":
        return e ^ 1, t
    if step in ("far", "near"):
        return (e ^ 4, t) if (e & 1) == (step == "far") else (e ^ 8, t)
    return (e, t ^ 1) if (e & 1) == (step == "late") else (e ^ 2, t)


def exchange(block, step):
    parts = lax.axis_size("tensor")
    perm = []
    for e in range(lax.axis_size("expert")):
        for t in range(parts):
            other = partner(step, e, t)
            perm.append((e * parts + t, other[0] * parts + other[1]))
    return lax.ppermute(block, AXES, perm)


STEPS = ("far", "near", "late", "early")
GATHER = (
    (22, ("near", "far", "early", "late")),
    (16, ("near", "early", "far", "late")),
    (18, ("far", "early", "late", "near")),
)
SCATTER = (
    (19, ("late", "early", "far", "near")),
    (18, ("near", "late", "early", "far")),
    (19, ("late", "early", "near", "far")),
)
GATHER_TURNS = (10, 1, 12, 10, 11, 2, 10, 11, 12, 10, 12, 11, 10, 10, 10, 12, 11, 11, 12, 11, 12)
SCATTER_TURNS = (0, 11, 12, 0, 2, 10, 1, 2, 10, 1, 0, 2, 1, 2, 11)
PACKED = 1


def chunks_of(width, plan):
    tiles, total = width // 128, sum(share for share, _ in plan)
    edges, at = [0], 0
    for share, _ in plan:
        at += share
        edges.append(128 * (tiles * at // total))
    return [(lo, hi, order) for lo, hi, (_, order) in zip(edges[:-1], edges[1:], plan)]


def gather_rows(tokens, packed, w_gate, w_up, chunks):
    count, width = tokens.shape
    blocks = [tokens[:, lo:hi] for lo, hi, _ in chunks]
    blocks[PACKED] = jnp.concatenate([blocks[PACKED], packed], axis=1)
    state = [[block.reshape(1, 1, 1, 1, count, -1), None, 0] for block in blocks]
    before = tokens
    gates, ups, spread = [0.0, 0.0], [0.0, 0.0], [None, None]

    def products(k, j, rows):
        lo, hi, _ = chunks[k]
        if k == PACKED:
            spread[j], rows = rows[:, hi - lo :], rows[:, : hi - lo]
        gates[j] = gates[j] + jnp.dot(rows, w_gate[lo:hi], preferred_element_type=jnp.float32)
        ups[j] = ups[j] + jnp.dot(rows, w_up[lo:hi], preferred_element_type=jnp.float32)
        return ups[j]

    for k in GATHER_TURNS:
        free, k = k >= 10, k % 10
        rows, arrived, done = state[k]
        order = chunks[k][2]
        if free:
            pass
        elif done > 0 and done != len(order) + 1:
            arrived, before = lax.optimization_barrier((arrived, before))
        elif done > 0:
            rows, before = lax.optimization_barrier((rows, before))
        if 0 < done <= len(order):
            rows = jnp.concatenate([rows, arrived], axis=STEPS.index(order[done - 1]))
            before = rows
        if done < len(order):
            arrived = exchange(rows, order[done])
        elif done == len(order):
            rows = rows.reshape(16 * count, -1)
            arrived = exchange(rows, "core")
        elif done == len(order) + 1:
            before = products(k, 0, rows)
        else:
            before = products(k, 1, arrived)
        state[k] = [rows, arrived, done + 1]
    return gates, ups, spread


def scatter_rows(hidden, w_down, chunks):
    def product(j, chunk):
        lo, hi, _ = chunk
        return jnp.dot(hidden[j], w_down[:, lo:hi], preferred_element_type=jnp.float32)

    state = [[exchange(product(1, chunk).astype(jnp.bfloat16), "core"), None, 0] for chunk in chunks]
    before = hidden[0]
    count = hidden[0].shape[0] // 16
    outs = [None] * len(chunks)
    for k in SCATTER_TURNS:
        free, k = k >= 10, k % 10
        arrived, mine, done = state[k]
        lo, hi, order = chunks[k]
        if not free:
            arrived, before = lax.optimization_barrier((arrived, before))
        if done == 0:
            total = product(0, chunks[k]) + arrived.astype(jnp.float32)
            total = total.reshape(2, 2, 2, 2, count, hi - lo).astype(jnp.bfloat16)
        else:
            total = (mine.astype(jnp.float32) + arrived.astype(jnp.float32)).astype(jnp.bfloat16)
        before = total
        if done == len(order):
            outs[k] = total.reshape(count, hi - lo)
            continue
        axis = STEPS.index(order[done])
        mine, other = lax.slice_in_dim(total, 0, 1, axis=axis), lax.slice_in_dim(total, 1, 2, axis=axis)
        state[k] = [exchange(other, order[done]), mine, done + 1]
    return jnp.concatenate(outs, axis=1)


def dense(tokens, expert_ids, gate_values, w_gate, w_up, w_down):
    experts = lax.axis_size("expert")
    count, width = tokens.shape
    weights = expert_weights(expert_ids, gate_values, experts)
    high = lax.reduce_precision(weights, 8, 7)
    packed = jnp.concatenate([high, weights - high], axis=1).astype(jnp.bfloat16)
    packed = jnp.pad(packed, ((0, 0), (0, -2 * experts % 128)))
    gates, ups, spread = gather_rows(tokens, packed, w_gate[0], w_up[0], chunks_of(width, GATHER))
    me = lax.axis_index("expert")
    column = jnp.arange(spread[0].shape[1], dtype=jnp.int32)
    named = (column == me) | (column == me + experts)
    hidden = []
    for gate, up, rows in zip(gates, ups, spread):
        scale = jnp.sum(jnp.where(named[None, :], rows.astype(jnp.float32), 0.0), axis=1, keepdims=True)
        hidden.append((scale * (jax.nn.silu(gate) * up)).astype(jnp.bfloat16))
    return scatter_rows(hidden, w_down[0], chunks_of(width, SCATTER))


def local(tokens, expert_ids, gate_values, w_gate, w_up, w_down):
    experts = lax.axis_size("expert")
    count, top = expert_ids.shape
    capacity = min(count, max(2, 2 * count * top // experts))
    if capacity < count or experts != 16 or lax.axis_size("tensor") != 2:
        return slotted(tokens, expert_ids, gate_values, w_gate, w_up, w_down, capacity)
    return dense(tokens, expert_ids, gate_values, w_gate, w_up, w_down)


def solution(mesh):
    return jax.shard_map(
        local,
        mesh=mesh,
        in_specs=(
            P(("expert", "tensor"), None),
            P(("expert", "tensor"), None),
            P(("expert", "tensor"), None),
            P("expert", None, "tensor"),
            P("expert", None, "tensor"),
            P("expert", "tensor", None),
        ),
        out_specs=P(("expert", "tensor"), None),
        check_vma=False,
    )
```

```python
import jax
import jax.numpy as jnp
from jax import lax
from jax.sharding import PartitionSpec as P

AXES = ("expert", "tensor")


def slot_places(expert_ids, experts, capacity):
    count = expert_ids.shape[0] * expert_ids.shape[1]
    flat = expert_ids.reshape(count)
    onehot = (flat[:, None] == jnp.arange(experts, dtype=jnp.int32)[None, :]).astype(jnp.int32)
    ranks = jnp.sum(jnp.cumsum(onehot, axis=0) * onehot, axis=1) - 1
    return flat * capacity + ranks


def dispatch_rows(tokens, places, experts, capacity, top):
    count = tokens.shape[0]
    table = (places[:, None] == jnp.arange(experts * capacity, dtype=jnp.int32)[None, :]).astype(
        jnp.bfloat16
    )
    table = jnp.sum(table.reshape(count, top, experts * capacity), axis=1)
    rows = jnp.einsum("ns,nd->sd", table, tokens, preferred_element_type=jnp.float32)
    return rows.astype(jnp.bfloat16).reshape(experts, capacity, tokens.shape[1])


def swiglu(rows, wg, wu):
    gate = jnp.dot(rows, wg, preferred_element_type=jnp.float32)
    up = jnp.dot(rows, wu, preferred_element_type=jnp.float32)
    return (jax.nn.silu(gate) * up).astype(jnp.bfloat16)


def slotted(tokens, expert_ids, gate_values, w_gate, w_up, w_down, capacity):
    experts = lax.axis_size("expert")
    count, top = expert_ids.shape
    width = tokens.shape[1]
    places = slot_places(expert_ids, experts, capacity)
    sending = dispatch_rows(tokens, places, experts, capacity, top)
    arrived = lax.all_to_all(sending, "expert", split_axis=0, concat_axis=0, tiled=True)
    rows = arrived.reshape(experts * capacity, width)
    hidden = swiglu(lax.all_gather(rows, "tensor", axis=0, tiled=True), w_gate[0], w_up[0])
    summed = lax.psum_scatter(
        jnp.dot(hidden, w_down[0], preferred_element_type=jnp.float32).astype(jnp.bfloat16),
        "tensor",
        scatter_dimension=0,
        tiled=True,
    )
    out_rows = summed.reshape(experts, capacity, width)
    returned = lax.all_to_all(out_rows, "expert", split_axis=0, concat_axis=0, tiled=True)
    picked = returned.reshape(experts * capacity, width)[places].reshape(count, top, width)
    mixed = jnp.sum(gate_values[:, :, None] * picked.astype(jnp.float32), axis=1)
    return mixed.astype(jnp.bfloat16)


def expert_weights(expert_ids, gate_values, experts):
    named = expert_ids[:, :, None] == jnp.arange(experts, dtype=jnp.int32)[None, None, :]
    return jnp.sum(jnp.where(named, gate_values[:, :, None], 0.0), axis=1)


def partner(step, e, t, turned):
    if step == "core":
        return e ^ 1, t
    if step in ("far", "near"):
        return (e ^ 8, t) if (step == "far") != (turned and e & 1 == 1) else (e ^ 4, t)
    return (e, t ^ 1) if (e & 1) == (step == "late") else (e ^ 2, t)


def exchange(block, step, turned=False):
    parts = lax.axis_size("tensor")
    perm = []
    for e in range(lax.axis_size("expert")):
        for t in range(parts):
            other = partner(step, e, t, turned)
            perm.append((e * parts + t, other[0] * parts + other[1]))
    return lax.ppermute(block, AXES, perm)


STEPS = ("far", "near", "late", "early")
GATHER = (
    (20, ("far", "early", "late", "near")),
    (24, ("far", "near", "early", "late")),
    (12, ("far", "near", "early", "late")),
)
SCATTER = (
    (17, ("late", "early", "far", "near")),
    (20, ("near", "late", "early", "far")),
    (19, ("late", "early", "near", "far")),
)
GATHER_TURNS = (10, 11, 12, 10, 12, 11, 10, 12, 11, 10, 12, 11, 12, 12, 12, 10, 10, 11, 11, 11, 10)
SCATTER_TURNS = (0, 1, 2, 0, 2, 0, 1, 0, 2, 1, 0, 2, 1, 2, 11)
PACKED = 1


def chunks_of(width, plan):
    tiles, total = width // 128, sum(share for share, _ in plan)
    edges, at = [0], 0
    for share, _ in plan:
        at += share
        edges.append(128 * (tiles * at // total))
    return [(lo, hi, order) for lo, hi, (_, order) in zip(edges[:-1], edges[1:], plan)]


def gather_rows(tokens, packed, w_gate, w_up, chunks):
    count, width = tokens.shape
    blocks = [tokens[:, lo:hi] for lo, hi, _ in chunks]
    blocks[PACKED] = jnp.concatenate([blocks[PACKED], packed], axis=1)
    state = [[block.reshape(1, 1, 1, 1, count, -1), None, 0] for block in blocks]
    before = tokens
    gates, ups, spread = [0.0, 0.0], [0.0, 0.0], [None, None]

    def products(k, j, rows):
        lo, hi, _ = chunks[k]
        if k == PACKED:
            spread[j], rows = rows[:, hi - lo :], rows[:, : hi - lo]
        gates[j] = gates[j] + jnp.dot(rows, w_gate[lo:hi], preferred_element_type=jnp.float32)
        ups[j] = ups[j] + jnp.dot(rows, w_up[lo:hi], preferred_element_type=jnp.float32)
        return ups[j]

    for k in GATHER_TURNS:
        free, k = k >= 10, k % 10
        rows, arrived, done = state[k]
        order = chunks[k][2]
        if free:
            pass
        elif done > 0 and done != len(order) + 1:
            arrived, before = lax.optimization_barrier((arrived, before))
        elif done > 0:
            rows, before = lax.optimization_barrier((rows, before))
        if 0 < done <= len(order):
            rows = jnp.concatenate([rows, arrived], axis=STEPS.index(order[done - 1]))
            before = rows
        if done < len(order):
            arrived = exchange(rows, order[done])
        elif done == len(order):
            rows = rows.reshape(16 * count, -1)
            arrived = exchange(rows, "core")
        elif done == len(order) + 1:
            before = products(k, 0, rows)
        else:
            before = products(k, 1, arrived)
        state[k] = [rows, arrived, done + 1]
    return gates, ups, spread


def scatter_rows(hidden, scale, w_down, chunks):
    core = lax.axis_index("expert") & 1

    def turn(rows, j):
        turned = rows.reshape(2, 2, -1, *rows.shape[1:]).swapaxes(0, 1).reshape(rows.shape)
        return jnp.where(core != j, turned, rows)

    hidden = [turn(rows, j) for j, rows in enumerate(hidden)]
    scale = [turn(rows, j) for j, rows in enumerate(scale)]

    def product(j, chunk):
        lo, hi, _ = chunk
        return scale[j][:, None] * jnp.dot(hidden[j], w_down[:, lo:hi], preferred_element_type=jnp.float32)

    state = [[exchange(product(1, chunk).astype(jnp.bfloat16), "core"), None, 0] for chunk in chunks]
    before = hidden[0]
    count = hidden[0].shape[0] // 16
    outs = [None] * len(chunks)
    for k in SCATTER_TURNS:
        free, k = k >= 10, k % 10
        arrived, mine, done = state[k]
        lo, hi, order = chunks[k]
        if not free:
            arrived, before = lax.optimization_barrier((arrived, before))
        if done == 0:
            total = product(0, chunks[k]) + arrived.astype(jnp.float32)
            total = total.reshape(2, 2, 2, 2, count, hi - lo).astype(jnp.bfloat16)
        else:
            total = (mine.astype(jnp.float32) + arrived.astype(jnp.float32)).astype(jnp.bfloat16)
        before = total
        if done == len(order):
            outs[k] = total.reshape(count, hi - lo)
            continue
        axis = STEPS.index(order[done])
        mine, other = lax.slice_in_dim(total, 0, 1, axis=axis), lax.slice_in_dim(total, 1, 2, axis=axis)
        state[k] = [exchange(other, order[done], True), mine, done + 1]
    return jnp.concatenate(outs, axis=1)


def dense(tokens, expert_ids, gate_values, w_gate, w_up, w_down):
    experts = lax.axis_size("expert")
    count, width = tokens.shape
    weights = expert_weights(expert_ids, gate_values, experts)
    high = lax.reduce_precision(weights, 8, 7)
    packed = jnp.concatenate([high, weights - high], axis=1).astype(jnp.bfloat16)
    packed = jnp.pad(packed, ((0, 0), (0, -2 * experts % 128)))
    gates, ups, spread = gather_rows(tokens, packed, w_gate[0], w_up[0], chunks_of(width, GATHER))
    hidden = [(jax.nn.silu(gate) * up).astype(jnp.bfloat16) for gate, up in zip(gates, ups)]
    me = lax.axis_index("expert")
    column = jnp.arange(spread[0].shape[1], dtype=jnp.int32)
    named = (column == me) | (column == me + experts)
    scale = [
        jnp.sum(jnp.where(named[None, :], rows.astype(jnp.float32), 0.0), axis=1)
        for rows in spread
    ]
    return scatter_rows(hidden, scale, w_down[0], chunks_of(width, SCATTER))


def local(tokens, expert_ids, gate_values, w_gate, w_up, w_down):
    experts = lax.axis_size("expert")
    count, top = expert_ids.shape
    capacity = min(count, max(2, 2 * count * top // experts))
    if capacity < count or experts != 16 or lax.axis_size("tensor") != 2:
        return slotted(tokens, expert_ids, gate_values, w_gate, w_up, w_down, capacity)
    return dense(tokens, expert_ids, gate_values, w_gate, w_up, w_down)


def solution(mesh):
    return jax.shard_map(
        local,
        mesh=mesh,
        in_specs=(
            P(("expert", "tensor"), None),
            P(("expert", "tensor"), None),
            P(("expert", "tensor"), None),
            P("expert", None, "tensor"),
            P("expert", None, "tensor"),
            P("expert", "tensor", None),
        ),
        out_specs=P(("expert", "tensor"), None),
        check_vma=False,
    )
```

```python
import jax
import jax.numpy as jnp
from jax import lax
from jax.sharding import PartitionSpec as P

AXES = ("expert", "tensor")


def slot_places(expert_ids, experts, capacity):
    count = expert_ids.shape[0] * expert_ids.shape[1]
    flat = expert_ids.reshape(count)
    onehot = (flat[:, None] == jnp.arange(experts, dtype=jnp.int32)[None, :]).astype(jnp.int32)
    ranks = jnp.sum(jnp.cumsum(onehot, axis=0) * onehot, axis=1) - 1
    return flat * capacity + ranks


def dispatch_rows(tokens, places, experts, capacity, top):
    count = tokens.shape[0]
    table = (places[:, None] == jnp.arange(experts * capacity, dtype=jnp.int32)[None, :]).astype(
        jnp.bfloat16
    )
    table = jnp.sum(table.reshape(count, top, experts * capacity), axis=1)
    rows = jnp.einsum("ns,nd->sd", table, tokens, preferred_element_type=jnp.float32)
    return rows.astype(jnp.bfloat16).reshape(experts, capacity, tokens.shape[1])


def swiglu(rows, wg, wu):
    gate = jnp.dot(rows, wg, preferred_element_type=jnp.float32)
    up = jnp.dot(rows, wu, preferred_element_type=jnp.float32)
    return (jax.nn.silu(gate) * up).astype(jnp.bfloat16)


def slotted(tokens, expert_ids, gate_values, w_gate, w_up, w_down, capacity):
    experts = lax.axis_size("expert")
    count, top = expert_ids.shape
    width = tokens.shape[1]
    places = slot_places(expert_ids, experts, capacity)
    sending = dispatch_rows(tokens, places, experts, capacity, top)
    arrived = lax.all_to_all(sending, "expert", split_axis=0, concat_axis=0, tiled=True)
    rows = arrived.reshape(experts * capacity, width)
    hidden = swiglu(lax.all_gather(rows, "tensor", axis=0, tiled=True), w_gate[0], w_up[0])
    summed = lax.psum_scatter(
        jnp.dot(hidden, w_down[0], preferred_element_type=jnp.float32).astype(jnp.bfloat16),
        "tensor",
        scatter_dimension=0,
        tiled=True,
    )
    out_rows = summed.reshape(experts, capacity, width)
    returned = lax.all_to_all(out_rows, "expert", split_axis=0, concat_axis=0, tiled=True)
    picked = returned.reshape(experts * capacity, width)[places].reshape(count, top, width)
    mixed = jnp.sum(gate_values[:, :, None] * picked.astype(jnp.float32), axis=1)
    return mixed.astype(jnp.bfloat16)


def expert_weights(expert_ids, gate_values, experts):
    named = expert_ids[:, :, None] == jnp.arange(experts, dtype=jnp.int32)[None, None, :]
    return jnp.sum(jnp.where(named, gate_values[:, :, None], 0.0), axis=1)


def partner(step, e, t):
    if step == "core":
        return e ^ 1, t
    if step in ("far", "near"):
        return (e ^ 4, t) if (e & 1) == (step == "far") else (e ^ 8, t)
    return (e, t ^ 1) if (e & 1) == (step == "late") else (e ^ 2, t)


def exchange(block, step):
    parts = lax.axis_size("tensor")
    perm = []
    for e in range(lax.axis_size("expert")):
        for t in range(parts):
            other = partner(step, e, t)
            perm.append((e * parts + t, other[0] * parts + other[1]))
    return lax.ppermute(block, AXES, perm)


STEPS = ("far", "near", "late", "early")
GATHER = (
    (22, ("near", "far", "early", "late")),
    (16, ("near", "late", "far", "early")),
    (18, ("far", "early", "late", "near")),
)
SCATTER = (
    (19, ("late", "early", "far", "near")),
    (18, ("near", "late", "early", "far")),
    (19, ("early", "late", "near", "far")),
)
GATHER_TURNS = (10, 1, 12, 10, 11, 2, 10, 11, 12, 10, 12, 11, 10, 10, 10, 12, 11, 11, 12, 11, 12)
SCATTER_TURNS = (0, 11, 2, 0, 2, 0, 1, 2, 0, 1, 2, 0, 1, 2, 11)
PACKED = 2


def chunks_of(width, plan):
    tiles, total = width // 128, sum(share for share, _ in plan)
    edges, at = [0], 0
    for share, _ in plan:
        at += share
        edges.append(128 * (tiles * at // total))
    return [(lo, hi, order) for lo, hi, (_, order) in zip(edges[:-1], edges[1:], plan)]


def gather_rows(tokens, packed, w_gate, w_up, chunks):
    count, width = tokens.shape
    blocks = [tokens[:, lo:hi] for lo, hi, _ in chunks]
    blocks[PACKED] = jnp.concatenate([blocks[PACKED], packed], axis=1)
    state = [[block.reshape(1, 1, 1, 1, count, -1), None, 0] for block in blocks]
    before = tokens
    gates, ups, spread = [0.0, 0.0], [0.0, 0.0], [None, None]

    def products(k, j, rows):
        lo, hi, _ = chunks[k]
        if k == PACKED:
            spread[j], rows = rows[:, hi - lo :], rows[:, : hi - lo]
        gates[j] = gates[j] + jnp.dot(rows, w_gate[lo:hi], preferred_element_type=jnp.float32)
        ups[j] = ups[j] + jnp.dot(rows, w_up[lo:hi], preferred_element_type=jnp.float32)
        return ups[j]

    for k in GATHER_TURNS:
        free, k = k >= 10, k % 10
        rows, arrived, done = state[k]
        order = chunks[k][2]
        if free:
            pass
        elif done > 0 and done != len(order) + 1:
            arrived, before = lax.optimization_barrier((arrived, before))
        elif done > 0:
            rows, before = lax.optimization_barrier((rows, before))
        if 0 < done <= len(order):
            rows = jnp.concatenate([rows, arrived], axis=STEPS.index(order[done - 1]))
            before = rows
        if done < len(order):
            arrived = exchange(rows, order[done])
        elif done == len(order):
            rows = rows.reshape(16 * count, -1)
            arrived = exchange(rows, "core")
        elif done == len(order) + 1:
            before = products(k, 0, rows)
        else:
            before = products(k, 1, arrived)
        state[k] = [rows, arrived, done + 1]
    return gates, ups, spread


def scatter_rows(hidden, scale, w_down, chunks):
    def product(j, chunk):
        lo, hi, _ = chunk
        return scale[j] * jnp.dot(hidden[j], w_down[:, lo:hi], preferred_element_type=jnp.float32)

    state = [[exchange(product(1, chunk).astype(jnp.bfloat16), "core"), None, 0] for chunk in chunks]
    before = hidden[0]
    count = hidden[0].shape[0] // 16
    outs = [None] * len(chunks)
    for k in SCATTER_TURNS:
        free, k = k >= 10, k % 10
        arrived, mine, done = state[k]
        lo, hi, order = chunks[k]
        if not free:
            arrived, before = lax.optimization_barrier((arrived, before))
        if done == 0:
            total = product(0, chunks[k]) + arrived.astype(jnp.float32)
            total = total.reshape(2, 2, 2, 2, count, hi - lo).astype(jnp.bfloat16)
        else:
            total = (mine.astype(jnp.float32) + arrived.astype(jnp.float32)).astype(jnp.bfloat16)
        before = total
        if done == len(order):
            outs[k] = total.reshape(count, hi - lo)
            continue
        axis = STEPS.index(order[done])
        mine, other = lax.slice_in_dim(total, 0, 1, axis=axis), lax.slice_in_dim(total, 1, 2, axis=axis)
        state[k] = [exchange(other, order[done]), mine, done + 1]
    return jnp.concatenate(outs, axis=1)


def dense(tokens, expert_ids, gate_values, w_gate, w_up, w_down):
    experts = lax.axis_size("expert")
    count, width = tokens.shape
    weights = expert_weights(expert_ids, gate_values, experts)
    high = lax.reduce_precision(weights, 8, 7)
    packed = jnp.concatenate([high, weights - high], axis=1).astype(jnp.bfloat16)
    packed = jnp.pad(packed, ((0, 0), (0, -2 * experts % 128)))
    gates, ups, spread = gather_rows(tokens, packed, w_gate[0], w_up[0], chunks_of(width, GATHER))
    hidden = [(jax.nn.silu(gate) * up).astype(jnp.bfloat16) for gate, up in zip(gates, ups)]
    me = lax.axis_index("expert")
    column = jnp.arange(spread[0].shape[1], dtype=jnp.int32)
    named = (column == me) | (column == me + experts)
    scale = [
        jnp.sum(jnp.where(named[None, :], rows.astype(jnp.float32), 0.0), axis=1, keepdims=True)
        for rows in spread
    ]
    return scatter_rows(hidden, scale, w_down[0], chunks_of(width, SCATTER))


def local(tokens, expert_ids, gate_values, w_gate, w_up, w_down):
    experts = lax.axis_size("expert")
    count, top = expert_ids.shape
    capacity = min(count, max(2, 2 * count * top // experts))
    if capacity < count or experts != 16 or lax.axis_size("tensor") != 2:
        return slotted(tokens, expert_ids, gate_values, w_gate, w_up, w_down, capacity)
    return dense(tokens, expert_ids, gate_values, w_gate, w_up, w_down)


def solution(mesh):
    return jax.shard_map(
        local,
        mesh=mesh,
        in_specs=(
            P(("expert", "tensor"), None),
            P(("expert", "tensor"), None),
            P(("expert", "tensor"), None),
            P("expert", None, "tensor"),
            P("expert", None, "tensor"),
            P("expert", "tensor", None),
        ),
        out_specs=P(("expert", "tensor"), None),
        check_vma=False,
    )
```

```python
import jax
import jax.numpy as jnp
from jax import lax
from jax.sharding import PartitionSpec as P

AXES = ("expert", "tensor")


def slot_places(expert_ids, experts, capacity):
    count = expert_ids.shape[0] * expert_ids.shape[1]
    flat = expert_ids.reshape(count)
    onehot = (flat[:, None] == jnp.arange(experts, dtype=jnp.int32)[None, :]).astype(jnp.int32)
    ranks = jnp.sum(jnp.cumsum(onehot, axis=0) * onehot, axis=1) - 1
    return flat * capacity + ranks


def dispatch_rows(tokens, places, experts, capacity, top):
    count = tokens.shape[0]
    table = (places[:, None] == jnp.arange(experts * capacity, dtype=jnp.int32)[None, :]).astype(
        jnp.bfloat16
    )
    table = jnp.sum(table.reshape(count, top, experts * capacity), axis=1)
    rows = jnp.einsum("ns,nd->sd", table, tokens, preferred_element_type=jnp.float32)
    return rows.astype(jnp.bfloat16).reshape(experts, capacity, tokens.shape[1])


def swiglu(rows, wg, wu):
    gate = jnp.dot(rows, wg, preferred_element_type=jnp.float32)
    up = jnp.dot(rows, wu, preferred_element_type=jnp.float32)
    return (jax.nn.silu(gate) * up).astype(jnp.bfloat16)


def slotted(tokens, expert_ids, gate_values, w_gate, w_up, w_down, capacity):
    experts = lax.axis_size("expert")
    count, top = expert_ids.shape
    width = tokens.shape[1]
    places = slot_places(expert_ids, experts, capacity)
    sending = dispatch_rows(tokens, places, experts, capacity, top)
    arrived = lax.all_to_all(sending, "expert", split_axis=0, concat_axis=0, tiled=True)
    rows = arrived.reshape(experts * capacity, width)
    hidden = swiglu(lax.all_gather(rows, "tensor", axis=0, tiled=True), w_gate[0], w_up[0])
    summed = lax.psum_scatter(
        jnp.dot(hidden, w_down[0], preferred_element_type=jnp.float32).astype(jnp.bfloat16),
        "tensor",
        scatter_dimension=0,
        tiled=True,
    )
    out_rows = summed.reshape(experts, capacity, width)
    returned = lax.all_to_all(out_rows, "expert", split_axis=0, concat_axis=0, tiled=True)
    picked = returned.reshape(experts * capacity, width)[places].reshape(count, top, width)
    mixed = jnp.sum(gate_values[:, :, None] * picked.astype(jnp.float32), axis=1)
    return mixed.astype(jnp.bfloat16)


def expert_weights(expert_ids, gate_values, experts):
    named = expert_ids[:, :, None] == jnp.arange(experts, dtype=jnp.int32)[None, None, :]
    return jnp.sum(jnp.where(named, gate_values[:, :, None], 0.0), axis=1)


def partner(step, e, t):
    if step == "core":
        return e ^ 1, t
    if step in ("far", "near"):
        return (e ^ 4, t) if (e & 1) == (step == "far") else (e ^ 8, t)
    return (e, t ^ 1) if (e & 1) == (step == "late") else (e ^ 2, t)


def exchange(block, step):
    parts = lax.axis_size("tensor")
    perm = []
    for e in range(lax.axis_size("expert")):
        for t in range(parts):
            other = partner(step, e, t)
            perm.append((e * parts + t, other[0] * parts + other[1]))
    return lax.ppermute(block, AXES, perm)


STEPS = ("far", "near", "late", "early")
GATHER = (
    (22, ("near", "far", "early", "late")),
    (16, ("near", "early", "far", "late")),
    (18, ("far", "early", "late", "near")),
)
SCATTER = (
    (19, ("late", "early", "far", "near")),
    (18, ("near", "late", "early", "far")),
    (19, ("late", "early", "near", "far")),
)
GATHER_TURNS = (10, 1, 12, 10, 11, 2, 10, 11, 12, 10, 12, 11, 10, 10, 10, 12, 11, 11, 12, 11, 12)
SCATTER_TURNS = (0, 11, 2, 0, 2, 0, 1, 2, 0, 1, 2, 0, 1, 2, 11)
PACKED = 0


def chunks_of(width, plan):
    tiles, total = width // 128, sum(share for share, _ in plan)
    edges, at = [0], 0
    for share, _ in plan:
        at += share
        edges.append(128 * (tiles * at // total))
    return [(lo, hi, order) for lo, hi, (_, order) in zip(edges[:-1], edges[1:], plan)]


def gather_rows(tokens, packed, w_gate, w_up, chunks):
    count, width = tokens.shape
    blocks = [tokens[:, lo:hi] for lo, hi, _ in chunks]
    blocks[PACKED] = jnp.concatenate([blocks[PACKED], packed], axis=1)
    state = [[block.reshape(1, 1, 1, 1, count, -1), None, 0] for block in blocks]
    before = tokens
    gates, ups, spread = [0.0, 0.0], [0.0, 0.0], [None, None]

    def products(k, j, rows):
        lo, hi, _ = chunks[k]
        if k == PACKED:
            spread[j], rows = rows[:, hi - lo :], rows[:, : hi - lo]
        gates[j] = gates[j] + jnp.dot(rows, w_gate[lo:hi], preferred_element_type=jnp.float32)
        ups[j] = ups[j] + jnp.dot(rows, w_up[lo:hi], preferred_element_type=jnp.float32)
        return ups[j]

    for k in GATHER_TURNS:
        free, k = k >= 10, k % 10
        rows, arrived, done = state[k]
        order = chunks[k][2]
        if free:
            pass
        elif done > 0 and done != len(order) + 1:
            arrived, before = lax.optimization_barrier((arrived, before))
        elif done > 0:
            rows, before = lax.optimization_barrier((rows, before))
        if 0 < done <= len(order):
            rows = jnp.concatenate([rows, arrived], axis=STEPS.index(order[done - 1]))
            before = rows
        if done < len(order):
            arrived = exchange(rows, order[done])
        elif done == len(order):
            rows = rows.reshape(16 * count, -1)
            arrived = exchange(rows, "core")
        elif done == len(order) + 1:
            before = products(k, 0, rows)
        else:
            before = products(k, 1, arrived)
        state[k] = [rows, arrived, done + 1]
    return gates, ups, spread


def scatter_rows(hidden, scale, w_down, chunks):
    def product(j, chunk):
        lo, hi, _ = chunk
        return scale[j] * jnp.dot(hidden[j], w_down[:, lo:hi], preferred_element_type=jnp.float32)

    state = [[exchange(product(1, chunk).astype(jnp.bfloat16), "core"), None, 0] for chunk in chunks]
    before = hidden[0]
    count = hidden[0].shape[0] // 16
    outs = [None] * len(chunks)
    for k in SCATTER_TURNS:
        free, k = k >= 10, k % 10
        arrived, mine, done = state[k]
        lo, hi, order = chunks[k]
        if not free:
            arrived, before = lax.optimization_barrier((arrived, before))
        if done == 0:
            total = product(0, chunks[k]) + arrived.astype(jnp.float32)
            total = total.reshape(2, 2, 2, 2, count, hi - lo).astype(jnp.bfloat16)
        else:
            total = (mine.astype(jnp.float32) + arrived.astype(jnp.float32)).astype(jnp.bfloat16)
        before = total
        if done == len(order):
            outs[k] = total.reshape(count, hi - lo)
            continue
        axis = STEPS.index(order[done])
        mine, other = lax.slice_in_dim(total, 0, 1, axis=axis), lax.slice_in_dim(total, 1, 2, axis=axis)
        state[k] = [exchange(other, order[done]), mine, done + 1]
    return jnp.concatenate(outs, axis=1)


def dense(tokens, expert_ids, gate_values, w_gate, w_up, w_down):
    experts = lax.axis_size("expert")
    count, width = tokens.shape
    weights = expert_weights(expert_ids, gate_values, experts)
    high = lax.reduce_precision(weights, 8, 7)
    packed = jnp.concatenate([high, weights - high], axis=1).astype(jnp.bfloat16)
    packed = jnp.pad(packed, ((0, 0), (0, -2 * experts % 128)))
    gates, ups, spread = gather_rows(tokens, packed, w_gate[0], w_up[0], chunks_of(width, GATHER))
    hidden = [(jax.nn.silu(gate) * up).astype(jnp.bfloat16) for gate, up in zip(gates, ups)]
    me = lax.axis_index("expert")
    column = jnp.arange(spread[0].shape[1], dtype=jnp.int32)
    named = (column == me) | (column == me + experts)
    scale = [
        jnp.sum(jnp.where(named[None, :], rows.astype(jnp.float32), 0.0), axis=1, keepdims=True)
        for rows in spread
    ]
    return scatter_rows(hidden, scale, w_down[0], chunks_of(width, SCATTER))


def local(tokens, expert_ids, gate_values, w_gate, w_up, w_down):
    experts = lax.axis_size("expert")
    count, top = expert_ids.shape
    capacity = min(count, max(2, 2 * count * top // experts))
    if capacity < count or experts != 16 or lax.axis_size("tensor") != 2:
        return slotted(tokens, expert_ids, gate_values, w_gate, w_up, w_down, capacity)
    return dense(tokens, expert_ids, gate_values, w_gate, w_up, w_down)


def solution(mesh):
    return jax.shard_map(
        local,
        mesh=mesh,
        in_specs=(
            P(("expert", "tensor"), None),
            P(("expert", "tensor"), None),
            P(("expert", "tensor"), None),
            P("expert", None, "tensor"),
            P("expert", None, "tensor"),
            P("expert", "tensor", None),
        ),
        out_specs=P(("expert", "tensor"), None),
        check_vma=False,
    )
```

```python
import jax
import jax.numpy as jnp
from jax import lax
from jax.sharding import PartitionSpec as P

AXES = ("expert", "tensor")


def slot_places(expert_ids, experts, capacity):
    count = expert_ids.shape[0] * expert_ids.shape[1]
    flat = expert_ids.reshape(count)
    onehot = (flat[:, None] == jnp.arange(experts, dtype=jnp.int32)[None, :]).astype(jnp.int32)
    ranks = jnp.sum(jnp.cumsum(onehot, axis=0) * onehot, axis=1) - 1
    return flat * capacity + ranks


def dispatch_rows(tokens, places, experts, capacity, top):
    count = tokens.shape[0]
    table = (places[:, None] == jnp.arange(experts * capacity, dtype=jnp.int32)[None, :]).astype(
        jnp.bfloat16
    )
    table = jnp.sum(table.reshape(count, top, experts * capacity), axis=1)
    rows = jnp.einsum("ns,nd->sd", table, tokens, preferred_element_type=jnp.float32)
    return rows.astype(jnp.bfloat16).reshape(experts, capacity, tokens.shape[1])


def swiglu(rows, wg, wu):
    gate = jnp.dot(rows, wg, preferred_element_type=jnp.float32)
    up = jnp.dot(rows, wu, preferred_element_type=jnp.float32)
    return (jax.nn.silu(gate) * up).astype(jnp.bfloat16)


def slotted(tokens, expert_ids, gate_values, w_gate, w_up, w_down, capacity):
    experts = lax.axis_size("expert")
    count, top = expert_ids.shape
    width = tokens.shape[1]
    places = slot_places(expert_ids, experts, capacity)
    sending = dispatch_rows(tokens, places, experts, capacity, top)
    arrived = lax.all_to_all(sending, "expert", split_axis=0, concat_axis=0, tiled=True)
    rows = arrived.reshape(experts * capacity, width)
    hidden = swiglu(lax.all_gather(rows, "tensor", axis=0, tiled=True), w_gate[0], w_up[0])
    summed = lax.psum_scatter(
        jnp.dot(hidden, w_down[0], preferred_element_type=jnp.float32).astype(jnp.bfloat16),
        "tensor",
        scatter_dimension=0,
        tiled=True,
    )
    out_rows = summed.reshape(experts, capacity, width)
    returned = lax.all_to_all(out_rows, "expert", split_axis=0, concat_axis=0, tiled=True)
    picked = returned.reshape(experts * capacity, width)[places].reshape(count, top, width)
    mixed = jnp.sum(gate_values[:, :, None] * picked.astype(jnp.float32), axis=1)
    return mixed.astype(jnp.bfloat16)


def expert_weights(expert_ids, gate_values, experts):
    named = expert_ids[:, :, None] == jnp.arange(experts, dtype=jnp.int32)[None, None, :]
    return jnp.sum(jnp.where(named, gate_values[:, :, None], 0.0), axis=1)


def partner(step, e, t):
    if step == "core":
        return e ^ 1, t
    if step in ("far", "near"):
        return (e ^ 4, t) if (e & 1) == (step == "far") else (e ^ 8, t)
    return (e, t ^ 1) if (e & 1) == (step == "late") else (e ^ 2, t)


def exchange(block, step):
    parts = lax.axis_size("tensor")
    perm = []
    for e in range(lax.axis_size("expert")):
        for t in range(parts):
            other = partner(step, e, t)
            perm.append((e * parts + t, other[0] * parts + other[1]))
    return lax.ppermute(block, AXES, perm)


STEPS = ("far", "near", "late", "early")
GATHER = (
    (22, ("near", "far", "early", "late")),
    (16, ("near", "late", "far", "early")),
    (18, ("far", "early", "late", "near")),
)
SCATTER = (
    (19, ("late", "early", "far", "near")),
    (18, ("near", "late", "early", "far")),
    (19, ("early", "late", "near", "far")),
)
GATHER_TURNS = (10, 1, 12, 10, 11, 2, 10, 11, 12, 10, 12, 11, 10, 10, 10, 12, 11, 11, 12, 11, 12)
SCATTER_TURNS = (0, 11, 2, 0, 2, 0, 1, 2, 0, 1, 2, 0, 1, 2, 11)
PACKED = 1


def chunks_of(width, plan):
    tiles, total = width // 128, sum(share for share, _ in plan)
    edges, at = [0], 0
    for share, _ in plan:
        at += share
        edges.append(128 * (tiles * at // total))
    return [(lo, hi, order) for lo, hi, (_, order) in zip(edges[:-1], edges[1:], plan)]


def gather_rows(tokens, packed, w_gate, w_up, chunks):
    count, width = tokens.shape
    blocks = [tokens[:, lo:hi] for lo, hi, _ in chunks]
    blocks[PACKED] = jnp.concatenate([blocks[PACKED], packed], axis=1)
    state = [[block.reshape(1, 1, 1, 1, count, -1), None, 0] for block in blocks]
    before = tokens
    gates, ups, spread = [0.0, 0.0], [0.0, 0.0], [None, None]

    def products(k, j, rows):
        lo, hi, _ = chunks[k]
        if k == PACKED:
            spread[j], rows = rows[:, hi - lo :], rows[:, : hi - lo]
        gates[j] = gates[j] + jnp.dot(rows, w_gate[lo:hi], preferred_element_type=jnp.float32)
        ups[j] = ups[j] + jnp.dot(rows, w_up[lo:hi], preferred_element_type=jnp.float32)
        return ups[j]

    for k in GATHER_TURNS:
        free, k = k >= 10, k % 10
        rows, arrived, done = state[k]
        order = chunks[k][2]
        if free:
            pass
        elif done > 0 and done != len(order) + 1:
            arrived, before = lax.optimization_barrier((arrived, before))
        elif done > 0:
            rows, before = lax.optimization_barrier((rows, before))
        if 0 < done <= len(order):
            rows = jnp.concatenate([rows, arrived], axis=STEPS.index(order[done - 1]))
            before = rows
        if done < len(order):
            arrived = exchange(rows, order[done])
        elif done == len(order):
            rows = rows.reshape(16 * count, -1)
            arrived = exchange(rows, "core")
        elif done == len(order) + 1:
            before = products(k, 0, rows)
        else:
            before = products(k, 1, arrived)
        state[k] = [rows, arrived, done + 1]
    return gates, ups, spread


def scatter_rows(hidden, scale, w_down, chunks):
    def product(j, chunk):
        lo, hi, _ = chunk
        return scale[j] * jnp.dot(hidden[j], w_down[:, lo:hi], preferred_element_type=jnp.float32)

    state = [[exchange(product(1, chunk).astype(jnp.bfloat16), "core"), None, 0] for chunk in chunks]
    before = hidden[0]
    count = hidden[0].shape[0] // 16
    outs = [None] * len(chunks)
    for k in SCATTER_TURNS:
        free, k = k >= 10, k % 10
        arrived, mine, done = state[k]
        lo, hi, order = chunks[k]
        if not free:
            arrived, before = lax.optimization_barrier((arrived, before))
        if done == 0:
            total = product(0, chunks[k]) + arrived.astype(jnp.float32)
            total = total.reshape(2, 2, 2, 2, count, hi - lo).astype(jnp.bfloat16)
        else:
            total = (mine.astype(jnp.float32) + arrived.astype(jnp.float32)).astype(jnp.bfloat16)
        before = total
        if done == len(order):
            outs[k] = total.reshape(count, hi - lo)
            continue
        axis = STEPS.index(order[done])
        mine, other = lax.slice_in_dim(total, 0, 1, axis=axis), lax.slice_in_dim(total, 1, 2, axis=axis)
        state[k] = [exchange(other, order[done]), mine, done + 1]
    return jnp.concatenate(outs, axis=1)


def dense(tokens, expert_ids, gate_values, w_gate, w_up, w_down):
    experts = lax.axis_size("expert")
    count, width = tokens.shape
    weights = expert_weights(expert_ids, gate_values, experts)
    high = lax.reduce_precision(weights, 8, 7)
    packed = jnp.concatenate([high, weights - high], axis=1).astype(jnp.bfloat16)
    packed = jnp.pad(packed, ((0, 0), (0, -2 * experts % 128)))
    gates, ups, spread = gather_rows(tokens, packed, w_gate[0], w_up[0], chunks_of(width, GATHER))
    hidden = [(jax.nn.silu(gate) * up).astype(jnp.bfloat16) for gate, up in zip(gates, ups)]
    me = lax.axis_index("expert")
    column = jnp.arange(spread[0].shape[1], dtype=jnp.int32)
    named = (column == me) | (column == me + experts)
    scale = [
        jnp.sum(jnp.where(named[None, :], rows.astype(jnp.float32), 0.0), axis=1, keepdims=True)
        for rows in spread
    ]
    return scatter_rows(hidden, scale, w_down[0], chunks_of(width, SCATTER))


def local(tokens, expert_ids, gate_values, w_gate, w_up, w_down):
    experts = lax.axis_size("expert")
    count, top = expert_ids.shape
    capacity = min(count, max(2, 2 * count * top // experts))
    if capacity < count or experts != 16 or lax.axis_size("tensor") != 2:
        return slotted(tokens, expert_ids, gate_values, w_gate, w_up, w_down, capacity)
    return dense(tokens, expert_ids, gate_values, w_gate, w_up, w_down)


def solution(mesh):
    return jax.shard_map(
        local,
        mesh=mesh,
        in_specs=(
            P(("expert", "tensor"), None),
            P(("expert", "tensor"), None),
            P(("expert", "tensor"), None),
            P("expert", None, "tensor"),
            P("expert", None, "tensor"),
            P("expert", "tensor", None),
        ),
        out_specs=P(("expert", "tensor"), None),
        check_vma=False,
    )
```
